512 devices in a mesh: row: 32 (over z, x_lo, core), col: 16 (over x_hi, y).
Axes of the slice: x: 4 (x_hi: 2, x_lo: 2; x = x_hi * 2 + x_lo), y: 8, z: 8, core: 2. Of those that a mesh axis runs over, the one named last changes fastest.
Arguments:
- right_side: float32 [1, 32, 1024, 512], P(None, 'row', 'col'), may hold values from -6 to 6
- prior_panel: bfloat16 [1, 32, 1, 16, 1024, 1024], P(None, 'row', None, 'col'), may hold values from -0.0625 to 0.0625
- prior_solved: bfloat16 [1, 16, 1024, 512], P(None, 'col'), may hold values from -6 to 6
- window_panel: bfloat16 [1, 32, 4, 1024, 1024], P(None, 'row', None, 'col'), may hold values from -0.09375 to 0.09375
- diag_inverse: bfloat16 [4, 1024, 1024], P(None, 'col'), as said below
Outputs:
- updated: float32 [1, 32, 1024, 512], P(None, 'row', 'col')
The draws below stay inside these ranges and needn't reach their ends.
Inputs may be any that keep to these rules, and one draw needn't show every extreme that they name: `diag_inverse`: lower triangular: entries above the diagonal of each block are zero; diagonal entries are positive.
All inputs are finite; a program needn't handle non-finite values.
Results may differ from the reference program's by a relative error of at most 0.022.
Values may be sent and summed in bfloat16 or wider, within the bound.
A program may use at most 128 MiB of HBM per device.

```python
import math
import jax
import jax.numpy as jnp
from jax import lax

NB = 1024
NRHS = 512
TICKS = 4
RPD = 1
PPD = 1
NPREV = 16
N_ROW = 32
N_COL = 16


def draw_diag_inverse(key, part):
    key = jax.random.fold_in(key, 11)
    under_key, scale_key = jax.random.split(key)
    under_part = jax.random.normal(under_key, (TICKS, NB, NB), jnp.float32) * NB ** (-0.5)
    diagonal_scales = jnp.exp(jax.random.uniform(scale_key, (TICKS, NB), jnp.float32, math.log(0.5), math.log(2.0)))
    row_index = lax.broadcasted_iota(jnp.int32, (NB, NB), 0)
    column_index = lax.broadcasted_iota(jnp.int32, (NB, NB), 1)
    lower_part = jnp.where(row_index > column_index, under_part, 0.0)
    diagonal_part = jnp.where(row_index == column_index, 1.0, 0.0) * diagonal_scales[:, :, None]
    return (lower_part + diagonal_part).astype(jnp.bfloat16)


def spiked(entries, rng, source, target, blocks, factor):
    owner, partner = [(jnp.arange(entries.shape[dim]) // (entries.shape[dim] // blocks)).reshape([-1 if axis == dim else 1 for axis in range(entries.ndim)]) for dim in (source, target)]
    chosen = jax.random.permutation(rng, blocks)[partner]
    strong = (owner == chosen) | (owner == (partner + blocks // 2) % blocks)
    return jnp.where(strong, factor * entries, entries)


def levels(own_key, extent, cuts, smallest, high):
    def one(dim, shards_of):
        steps = jax.random.uniform(jax.random.fold_in(jax.random.fold_in(own_key, 6), dim), (shards_of,), jnp.float32, smallest / len(cuts), high / len(cuts))
        return jnp.repeat(jnp.exp(steps), extent[dim] // shards_of).reshape((-1,) + (1,) * (len(extent) - dim - 1))

    factor_of = one(*cuts[0])
    for cut in cuts[1:]:
        factor_of = factor_of * one(*cut)
    return factor_of


def noise(own_key, shape, scale, limit, cuts=(), held_as=jnp.bfloat16):
    entries = scale * jax.random.normal(own_key, shape, jnp.float32)
    if cuts:
        entries = entries * levels(own_key, shape, cuts, -0.22, 0.18)
    return jnp.clip(entries, -limit, limit).astype(held_as)


def noise_with(stream_key, extent, width, most, cuts, heavy, held_as=jnp.bfloat16):
    result = width * jax.random.normal(stream_key, extent, jnp.float32)
    if cuts:
        result = result * levels(stream_key, extent, cuts, -0.22, 0.18)
    return jnp.clip(spiked(result, jax.random.fold_in(stream_key, 3), *heavy), -most, most).astype(held_as)


def setup_inputs(seed: int = 0) -> dict:
    arg_keys = jax.random.split(jax.random.key(seed), 6)
    right_side = noise(arg_keys[0], (RPD, N_ROW, NB, NRHS), 1.0, 6.0, ((1, 32), (2, 16)), jnp.float32)
    prior_panel = noise_with(arg_keys[1], (RPD, N_ROW, PPD, N_COL, NB, NB), (NPREV * NB) ** -0.5, 0.0625, ((1, 32), (3, 16)), (3, 4, 16, 2.0))
    prior_solved = noise(arg_keys[2], (PPD, N_COL, NB, NRHS), 1.0, 6.0, ((1, 16),))
    window_panel = noise(arg_keys[3], (RPD, N_ROW, TICKS, NB, NB), (TICKS * NB) ** -0.5, 0.09375, ((1, 32), (3, 16)))
    diag_inverse = draw_diag_inverse(jax.random.fold_in(arg_keys[5], 71), 0)
    return dict(right_side=right_side, prior_panel=prior_panel, prior_solved=prior_solved, window_panel=window_panel, diag_inverse=diag_inverse)


def reference(right_side, prior_panel, prior_solved, window_panel, diag_inverse):
    solved_groups = jnp.transpose(prior_solved, (1, 0, 2, 3)).reshape(N_COL, PPD * NB, NRHS).astype(jnp.float32)
    flat_panel = prior_panel.reshape(RPD * N_ROW, PPD, N_COL, NB, NB)

    def block_contribution(block):
        arranged = jnp.transpose(block, (1, 2, 0, 3)).reshape(N_COL, NB, PPD * NB).astype(jnp.float32)
        partial_sums = jnp.einsum('qxj,qjn->qxn', arranged, solved_groups, precision=lax.Precision.HIGHEST)
        rounded = partial_sums.astype(jnp.bfloat16).astype(jnp.float32)
        return jnp.sum(rounded, axis=0)

    prior = lax.map(block_contribution, flat_panel)
    pending = right_side.reshape(RPD * N_ROW, NB, NRHS) - prior
    window = window_panel.reshape(RPD * N_ROW, TICKS, NB, NB)
    block_ids = jnp.arange(RPD * N_ROW, dtype=jnp.int32)
    solved_list = []
    for tick_index in range(TICKS):
        waiting = pending[tick_index].astype(jnp.bfloat16)
        solved = jnp.dot(diag_inverse[tick_index], waiting, preferred_element_type=jnp.float32).astype(jnp.bfloat16)
        update = jnp.einsum('ixj,jn->ixn', window[:, tick_index].astype(jnp.float32), solved.astype(jnp.float32), precision=lax.Precision.HIGHEST)
        live = block_ids > tick_index
        pending = pending - jnp.where(live[:, None, None], update, jnp.float32(0.0))
        solved_list.append(solved.astype(jnp.float32))
    for tick_index in range(TICKS):
        pending = pending.at[tick_index].set(solved_list[tick_index])
    return pending.reshape(RPD, N_ROW, NB, NRHS)
```

```python
import functools

import jax
import jax.numpy as jnp
from jax import lax
from jax.experimental import pallas as pl
from jax.experimental.pallas import tpu as pltpu
from jax.sharding import PartitionSpec as P

MESH = pl.DeviceIdType.MESH
F32 = jnp.float32
BF16 = jnp.bfloat16
LEVEL = 4
LANES = 128


def nt_dot(a, b):
    return lax.dot_general(
        a, b, (((1,), (1,)), ((), ())), preferred_element_type=F32
    )


def kernel(
    nz,
    ncol,
    rhs_h,
    panel_h,
    prior_h,
    win_h,
    dinv_h,
    out_ref,
    rhs,
    panel,
    prior,
    win,
    dinv,
    sendb,
    recv1,
    pend,
    pt,
    sca,
    pin,
    acc,
    a1,
    a2,
    sz,
    wsrc,
    wl,
    wc,
    usum,
    ub,
    load_sem,
    rs_send,
    rs_recv,
    sa_send,
    sa_recv,
    sb_send,
    sb_recv,
    wr_send,
    wr_recv,
    wc_send,
    wc_recv,
    wl_send,
    wl_recv,
    a1_send,
    a1_recv,
    a2_send,
    a2_recv,
    z_send,
    z_recv,
    u_send,
    u_recv,
):
    row = lax.axis_index("row")
    col = lax.axis_index("col")
    zed = row // LEVEL
    cls = row % LEVEL
    ticks, rows, size = win.shape
    width = pin.shape[1]
    columns = rhs.shape[1]
    parity = col % 2

    loads = [
        pltpu.make_async_copy(src, dst, load_sem.at[i])
        for i, (src, dst) in enumerate(
            ((prior_h, prior), (panel_h, panel), (win_h, win), (dinv_h, dinv), (rhs_h, rhs))
        )
    ]
    for load in loads:
        load.start()

    def on_col(d):
        return (row, lax.rem(col + d, ncol))

    def on_z(d):
        return (lax.rem(zed + d, nz) * LEVEL + cls, col)

    def on_level(d):
        return (zed * LEVEL + lax.rem(cls + d, LEVEL), col)

    def remote(src, dst, send, recv, device):
        return pltpu.make_async_remote_copy(
            src_ref=src,
            dst_ref=dst,
            send_sem=send,
            recv_sem=recv,
            device_id=device,
            device_id_type=MESH,
        )

    def wait_for(ref, sem):
        pltpu.make_async_copy(ref, ref, sem).wait()

    barrier = pltpu.get_barrier_semaphore()

    def greet(where):
        def body(d, carry):
            pl.semaphore_signal(
                barrier, inc=1, device_id=where(d), device_id_type=MESH
            )
            return carry

        return body

    lax.fori_loop(1, ncol, greet(on_col), 0)
    lax.fori_loop(1, nz, greet(on_z), 0)
    lax.fori_loop(1, LEVEL, greet(on_level), 0)
    pl.semaphore_wait(barrier, (ncol - 1) + (nz - 1) + (LEVEL - 1))

    mine = jnp.maximum(cls - 1, 0)
    loads[2].wait()

    def relay(j, device):
        return remote(wc.at[mine, j], wc.at[mine, j], wr_send, wr_recv.at[j], device)

    half = nz // 2
    upward = (zed < half)
    downward = (zed == 0) | (zed > half + 1)
    for j in range(LEVEL - 1):

        @pl.when((j < cls) & (zed == 0))
        def _():
            wc[mine, j] = win[j]
            relay(j, on_z(1)).start()
            if nz > 2:
                relay(j, on_z(nz - 1)).start()

    loads[0].wait()
    loads[1].wait()
    per_block = 4 if ncol % 4 == 0 else ncol
    blocks = ncol // per_block
    first = col // per_block + 1

    def product(i, carry):
        block = lax.rem(first + i, blocks)
        start = pl.multiple_of(block * per_block * rows, per_block * rows)
        part = jnp.dot(
            panel[pl.ds(start, per_block * rows), :], prior[...], preferred_element_type=F32
        ).astype(BF16)
        for s in range(per_block):
            sendb[block * per_block + s] = part[s * rows : (s + 1) * rows]

        def send(s, inner):
            target = block * per_block + s

            @pl.when(target != col)
            def _():
                slot = lax.rem(target - col + ncol, ncol) - 1
                remote(
                    sendb.at[target], recv1.at[slot], rs_send, rs_recv, (row, target)
                ).start()

            return inner

        return lax.fori_loop(0, per_block, send, carry)

    lax.fori_loop(0, blocks, product, 0)

    for j in range(LEVEL - 1):

        @pl.when((j < cls) & (zed > 0))
        def _():
            wait_for(wc.at[mine, j], wr_recv.at[j])

        @pl.when((j < cls) & (zed > 0) & upward)
        def _():
            relay(j, on_z(1)).start()

        @pl.when((j < cls) & (zed > 0) & downward)
        def _():
            relay(j, on_z(nz - 1)).start()

        @pl.when(j < cls)
        def _():
            def share(d, carry):
                remote(
                    wc.at[mine, j], wc.at[mine, j], wc_send, wc_recv.at[mine, j], on_level(d)
                ).start()
                return carry

            lax.fori_loop(1, LEVEL, share, 0)

    @pl.when(zed == 0)
    def _():
        picks = (
            lax.broadcasted_iota(jnp.int32, (rows, size), 1)
            == lax.broadcasted_iota(jnp.int32, (rows, size), 0) + col * rows
        )
        for k in range(ticks):
            wsrc[k] = jnp.where(picks & (cls == k), 1.0, 0.0).astype(BF16)

    @pl.when(zed > 0)
    def _():
        wsrc[...] = win[...]

    def spread(d, carry):
        remote(wsrc, wl.at[:, cls], wl_send, wl_recv, on_level(d)).start()
        return carry

    lax.fori_loop(1, LEVEL, spread, 0)
    wl[:, cls] = wsrc[...]

    loads[4].wait()
    loads[3].wait()
    wait_for(recv1, rs_recv)
    total = sendb[col].astype(F32)
    for s in range(ncol - 1):
        total = total + recv1[s].astype(F32)
    pend[...] = rhs[...] - total

    @pl.when(zed == 0)
    def _():
        value = pend[...]
        for q in range(LEVEL):
            part = jnp.concatenate(
                [value[:, q * LANES : (q + 1) * LANES]] * 2, axis=0
            ).T.astype(BF16)
            for t in range(nz):
                pt[q, t] = part[t * width : (t + 1) * width]

        def send(d, carry):
            remote(pt.at[:, lax.rem(zed + d, nz)], sca, sa_send, sa_recv, on_z(d)).start()
            return carry

        lax.fori_loop(1, nz, send, 0)
        sca[...] = pt[:, 0]

    @pl.when(zed > 0)
    def _():
        wait_for(sca, sa_recv)

    def deal(d, carry):
        remote(
            sca.at[lax.rem(cls + d, LEVEL)], pin.at[cls], sb_send, sb_recv, on_level(d)
        ).start()
        return carry

    lax.fori_loop(1, LEVEL, deal, 0)
    pin[cls] = sca[cls]
    wait_for(pin.at[pl.ds(0, LEVEL - 1)], sb_recv)
    for k in range(ticks):
        acc[k] = pin[k].astype(F32)

    lane = lax.broadcasted_iota(jnp.int32, (width, LANES), 1)
    kept = (lane >= parity * rows) & (lane < parity * rows + rows)

    def twice(value):
        return jnp.concatenate([value, value], axis=1)

    def gather(buf, k, value, send, recv):
        buf[k, col] = jnp.where(kept, value, 0.0).astype(BF16)

        def body(d, carry):
            remote(buf.at[k, col], buf.at[k, col], send.at[k], recv.at[k], on_col(d)).start()
            return carry

        lax.fori_loop(1, ncol, body, 0)

    def whole(buf, k, recv):
        wait_for(buf.at[k, pl.ds(0, ncol - 1)], recv.at[k])
        return jnp.concatenate(
            [buf[k, 2 * p] + buf[k, 2 * p + 1] for p in range(ncol // 2)], axis=1
        )

    def update_row(k, later, solved):
        @pl.when(cls != later)
        def _():
            wait_for(wc.at[later - 1, k], wc_recv.at[later - 1, k])

        acc[later] = acc[later] - twice(nt_dot(solved, wc[later - 1, k]))

    def final(k):
        if k == 0:
            wait_for(wl.at[:, pl.ds(0, LEVEL - 1)], wl_recv)
        if nz > 1:
            wait_for(sz.at[k, pl.ds(0, (nz - 1) * width)], z_recv.at[k])
        part = nt_dot(wl[k].reshape(LEVEL * rows, size), sz[k])
        for q in range(LEVEL):
            piece = part[q * rows : (q + 1) * rows]
            usum[q] = piece if k == 0 else usum[q] + piece

    place = pl.multiple_of(zed * width, width)
    solved = None
    for k in range(ticks):
        gather(a1, k, acc[k], a1_send, a1_recv)
        if k > 0:
            for later in range(k + 1, ticks):
                update_row(k - 1, later, solved)
        waiting = whole(a1, k, a1_recv)
        gather(a2, k, twice(nt_dot(waiting, dinv[k])), a2_send, a2_recv)
        if k >= 2:
            final(k - 2)
        solved = whole(a2, k, a2_recv)
        sz[k, pl.ds(place, width), :] = solved

        def along(d, carry):
            part = sz.at[k, pl.ds(place, width), :]
            remote(part, part, z_send, z_recv.at[k], on_z(d)).start()
            return carry

        lax.fori_loop(1, nz, along, 0)
        if k + 1 < ticks:
            update_row(k, k + 1, solved)

    for k in range(max(ticks - 2, 0), ticks):
        final(k)

    def give(d, carry):
        remote(
            usum.at[lax.rem(cls + d, LEVEL)], ub.at[cls], u_send, u_recv, on_level(d)
        ).start()
        return carry

    lax.fori_loop(1, LEVEL, give, 0)
    ub[cls] = usum[cls]
    wait_for(ub.at[pl.ds(0, LEVEL - 1)], u_recv)
    for q in range(LEVEL):
        cut = slice(q * LANES, (q + 1) * LANES)
        out_ref[:, cut] = jnp.where(zed == 0, ub[q], pend[:, cut] - ub[q])

    wait_for(recv1, rs_send)
    wait_for(ub.at[pl.ds(0, LEVEL - 1)], u_send)
    wait_for(pin.at[pl.ds(0, LEVEL - 1)], sb_send)
    wait_for(wl.at[:, pl.ds(0, LEVEL - 1)], wl_send)
    for k in range(ticks):
        wait_for(a1.at[k, pl.ds(0, ncol - 1)], a1_send.at[k])
        wait_for(a2.at[k, pl.ds(0, ncol - 1)], a2_send.at[k])
        wait_for(sz.at[k, pl.ds(0, (nz - 1) * width)], z_send)

    @pl.when(zed == 0)
    def _():
        wait_for(pt.at[:, pl.ds(0, nz - 1)], sa_send)

    for j in range(LEVEL - 1):

        @pl.when((j < cls) & upward)
        def _():
            wait_for(wc.at[mine, j], wr_send)

        @pl.when((j < cls) & downward & (nz > 2))
        def _():
            wait_for(wc.at[mine, j], wr_send)

        @pl.when(j < cls)
        def _():
            wait_for(wc.at[pl.ds(0, LEVEL - 1), j], wc_send)


def per_device(right_side, prior_panel, prior_solved, window_panel, diag_inverse):
    rows, columns = right_side.shape[2:]
    size = prior_panel.shape[4]
    ticks = window_panel.shape[2]
    ncol = lax.axis_size("col")
    nz = lax.axis_size("row") // LEVEL
    width = LANES // nz
    dma = pltpu.SemaphoreType.DMA
    vmem = pltpu.VMEM
    out = pl.pallas_call(
        functools.partial(kernel, nz, ncol),
        out_shape=jax.ShapeDtypeStruct((rows, columns), F32),
        in_specs=[pl.BlockSpec(memory_space=pl.ANY)] * 5,
        out_specs=pl.BlockSpec(memory_space=pltpu.VMEM),
        scratch_shapes=[
            vmem((rows, columns), F32),
            vmem((size, size), BF16),
            vmem((size, columns), BF16),
            vmem((ticks, rows, size), BF16),
            vmem((ticks, rows, size), BF16),
            vmem((ncol, rows, columns), BF16),
            vmem((ncol - 1, rows, columns), BF16),
            vmem((rows, columns), F32),
            vmem((LEVEL, nz, width, LANES), BF16),
            vmem((LEVEL, width, LANES), BF16),
            vmem((LEVEL, width, LANES), BF16),
            vmem((ticks, width, LANES), F32),
            vmem((ticks, ncol, width, LANES), BF16),
            vmem((ticks, ncol, width, LANES), BF16),
            vmem((ticks, LANES, size), BF16),
            vmem((ticks, rows, size), BF16),
            vmem((ticks, LEVEL, rows, size), BF16),
            vmem((LEVEL - 1, LEVEL - 1, rows, size), BF16),
            vmem((LEVEL, rows, LANES), F32),
            vmem((LEVEL, rows, LANES), F32),
            dma((5,)),
            dma,
            dma,
            dma,
            dma,
            dma,
            dma,
            dma,
            dma((LEVEL - 1,)),
            dma,
            dma((LEVEL - 1, LEVEL - 1)),
            dma,
            dma,
            dma((ticks,)),
            dma((ticks,)),
            dma((ticks,)),
            dma((ticks,)),
            dma,
            dma((ticks,)),
            dma,
            dma,
        ],
        compiler_params=pltpu.CompilerParams(
            collective_id=0,
            has_side_effects=True,
            vmem_limit_bytes=40 * 1024 * 1024,
        ),
    )(
        right_side.reshape(rows, columns),
        prior_panel.reshape(size, size),
        prior_solved.reshape(size, columns),
        window_panel.reshape(ticks, rows, size),
        diag_inverse,
    )
    return out.reshape(right_side.shape)


def solution(mesh):
    return jax.shard_map(
        per_device,
        mesh=mesh,
        in_specs=(
            P(None, "row", "col", None),
            P(None, "row", None, "col", None, None),
            P(None, "col", None, None),
            P(None, "row", None, "col", None),
            P(None, "col", None),
        ),
        out_specs=P(None, "row", "col", None),
        check_vma=False,
    )
```

```python
import functools

import jax
import jax.numpy as jnp
from jax import lax
from jax.experimental import pallas as pl
from jax.experimental.pallas import tpu as pltpu
from jax.sharding import PartitionSpec as P

MESH = pl.DeviceIdType.MESH
F32 = jnp.float32
BF16 = jnp.bfloat16
LEVEL = 4
LANES = 128


def nt_dot(a, b):
    return lax.dot_general(
        a, b, (((1,), (1,)), ((), ())), preferred_element_type=F32
    )


def kernel(
    nz,
    ncol,
    rhs_h,
    panel_h,
    prior_h,
    win_h,
    dinv_h,
    out_ref,
    rhs,
    panel,
    prior,
    win,
    dinv,
    sendb,
    recv1,
    pend,
    pt,
    sca,
    pin,
    acc,
    a1,
    a2,
    sz,
    wsrc,
    wl,
    wc,
    usum,
    ub,
    load_sem,
    rs_send,
    rs_recv,
    sa_send,
    sa_recv,
    sb_send,
    sb_recv,
    wr_send,
    wr_recv,
    wc_send,
    wc_recv,
    wl_send,
    wl_recv,
    a1_send,
    a1_recv,
    a2_send,
    a2_recv,
    z_send,
    z_recv,
    u_send,
    u_recv,
):
    row = lax.axis_index("row")
    col = lax.axis_index("col")
    zed = row // LEVEL
    cls = row % LEVEL
    ticks, rows, size = win.shape
    width = pin.shape[1]
    columns = rhs.shape[1]
    parity = col % 2

    loads = [
        pltpu.make_async_copy(src, dst, load_sem.at[i])
        for i, (src, dst) in enumerate(
            ((prior_h, prior), (panel_h, panel), (win_h, win), (dinv_h, dinv), (rhs_h, rhs))
        )
    ]
    for load in loads:
        load.start()

    near = ncol // 2
    far = sorted(
        ((dx, dy) for dx in range(2) for dy in range(near) if dx or dy),
        key=lambda p: -(2 * p[0] + min(p[1], near - p[1])),
    )

    def on_col(dx, dy):
        return (row, lax.rem(col // near + dx, 2) * near + lax.rem(col + dy, near))

    def on_z(d):
        return (lax.rem(zed + d, nz) * LEVEL + cls, col)

    def on_level(d):
        return (zed * LEVEL + lax.rem(cls + d, LEVEL), col)

    def remote(src, dst, send, recv, device):
        return pltpu.make_async_remote_copy(
            src_ref=src,
            dst_ref=dst,
            send_sem=send,
            recv_sem=recv,
            device_id=device,
            device_id_type=MESH,
        )

    def wait_for(ref, sem):
        pltpu.make_async_copy(ref, ref, sem).wait()

    barrier = pltpu.get_barrier_semaphore()

    def greet(where):
        def body(d, carry):
            pl.semaphore_signal(
                barrier, inc=1, device_id=where(d), device_id_type=MESH
            )
            return carry

        return body

    for dx, dy in far:
        pl.semaphore_signal(
            barrier, inc=1, device_id=on_col(dx, dy), device_id_type=MESH
        )
    lax.fori_loop(1, nz, greet(on_z), 0)
    lax.fori_loop(1, LEVEL, greet(on_level), 0)
    pl.semaphore_wait(barrier, (ncol - 1) + (nz - 1) + (LEVEL - 1))

    mine = jnp.maximum(cls - 1, 0)
    loads[2].wait()

    def relay(j, device):
        return remote(wc.at[mine, j], wc.at[mine, j], wr_send, wr_recv.at[j], device)

    half = nz // 2
    upward = (zed < half)
    downward = (zed == 0) | (zed > half + 1)
    for j in range(LEVEL - 1):

        @pl.when((j < cls) & (zed == 0))
        def _():
            wc[mine, j] = win[j]
            relay(j, on_z(1)).start()
            if nz > 2:
                relay(j, on_z(nz - 1)).start()

    @pl.when(zed == 0)
    def _():
        picks = (
            lax.broadcasted_iota(jnp.int32, (rows, size), 1)
            == lax.broadcasted_iota(jnp.int32, (rows, size), 0) + col * rows
        )
        for k in range(ticks):
            wsrc[k] = jnp.where(picks & (cls == k), 1.0, 0.0).astype(BF16)

    @pl.when(zed > 0)
    def _():
        wsrc[...] = win[...]


    beyond = lax.rem(cls + 2, LEVEL)
    twin = cls + 1 - 2 * lax.rem(cls, 2)
    on_beyond = (zed * LEVEL + beyond, col)
    on_twin = (zed * LEVEL + twin, col)
    remote(wsrc, wl.at[:, cls], wl_send, wl_recv.at[0], on_beyond).start()
    remote(wsrc, wl.at[:, cls], wl_send, wl_recv.at[1], on_twin).start()
    wl[:, cls] = wsrc[...]

    def pass_on():
        there = wl.at[:, beyond]
        wait_for(there, wl_recv.at[0])
        remote(there, there, wl_send, wl_recv.at[2], on_twin).start()

    loads[0].wait()
    loads[1].wait()
    per_block = 4 if ncol % 4 == 0 else ncol
    blocks = ncol // per_block
    first = col // per_block + 1

    def product(i, carry):
        block = lax.rem(first + i, blocks)
        start = pl.multiple_of(block * per_block * rows, per_block * rows)
        part = jnp.dot(
            panel[pl.ds(start, per_block * rows), :], prior[...], preferred_element_type=F32
        ).astype(BF16)
        for s in range(per_block):
            sendb[block * per_block + s] = part[s * rows : (s + 1) * rows]

        def send(s, inner):
            target = block * per_block + s

            @pl.when(target != col)
            def _():
                slot = lax.rem(target - col + ncol, ncol) - 1
                remote(
                    sendb.at[target], recv1.at[slot], rs_send, rs_recv, (row, target)
                ).start()

            return inner

        return lax.fori_loop(0, per_block, send, carry)

    lax.fori_loop(0, blocks, product, 0)

    for j in range(LEVEL - 1):

        @pl.when((j < cls) & (zed > 0))
        def _():
            wait_for(wc.at[mine, j], wr_recv.at[j])

        @pl.when((j < cls) & (zed > 0) & upward)
        def _():
            relay(j, on_z(1)).start()

        @pl.when((j < cls) & (zed > 0) & downward)
        def _():
            relay(j, on_z(nz - 1)).start()

        @pl.when(j < cls)
        def _():
            def share(d, carry):
                remote(
                    wc.at[mine, j], wc.at[mine, j], wc_send, wc_recv.at[mine, j], on_level(d)
                ).start()
                return carry

            lax.fori_loop(1, LEVEL, share, 0)

    loads[4].wait()
    loads[3].wait()
    wait_for(recv1, rs_recv)
    total = sendb[col].astype(F32)
    for s in range(ncol - 1):
        total = total + recv1[s].astype(F32)
    pend[...] = rhs[...] - total

    @pl.when(zed == 0)
    def _():
        value = pend[...]
        for q in range(LEVEL):
            part = jnp.concatenate(
                [value[:, q * LANES : (q + 1) * LANES]] * 2, axis=0
            ).T.astype(BF16)
            for t in range(nz):
                pt[q, t] = part[t * width : (t + 1) * width]

        def send(d, carry):
            remote(pt.at[:, lax.rem(zed + d, nz)], sca, sa_send, sa_recv, on_z(d)).start()
            return carry

        lax.fori_loop(1, nz, send, 0)
        sca[...] = pt[:, 0]

    @pl.when(zed > 0)
    def _():
        wait_for(sca, sa_recv)

    def deal(d, carry):
        remote(
            sca.at[lax.rem(cls + d, LEVEL)], pin.at[cls], sb_send, sb_recv, on_level(d)
        ).start()
        return carry

    lax.fori_loop(1, LEVEL, deal, 0)
    pin[cls] = sca[cls]
    wait_for(pin.at[pl.ds(0, LEVEL - 1)], sb_recv)
    for k in range(ticks):
        acc[k] = pin[k].astype(F32)

    lane = lax.broadcasted_iota(jnp.int32, (width, LANES), 1)
    kept = (lane >= parity * rows) & (lane < parity * rows + rows)

    def twice(value):
        return jnp.concatenate([value, value], axis=1)

    def gather(buf, k, value, send, recv):
        buf[k, col] = jnp.where(kept, value, 0.0).astype(BF16)

        for dx, dy in far:
            remote(
                buf.at[k, col], buf.at[k, col], send.at[k], recv.at[k], on_col(dx, dy)
            ).start()

    def whole(buf, k, recv):
        wait_for(buf.at[k, pl.ds(0, ncol - 1)], recv.at[k])
        return jnp.concatenate(
            [buf[k, 2 * p] + buf[k, 2 * p + 1] for p in range(ncol // 2)], axis=1
        )

    def update_row(k, later, solved):
        @pl.when(cls != later)
        def _():
            wait_for(wc.at[later - 1, k], wc_recv.at[later - 1, k])

        acc[later] = acc[later] - twice(nt_dot(solved, wc[later - 1, k]))

    def final(k):
        if k == 0:
            for way in range(1, 3):
                wait_for(wsrc, wl_recv.at[way])
        if nz > 1:
            wait_for(sz.at[k, pl.ds(0, (nz - 1) * width)], z_recv.at[k])
        part = nt_dot(wl[k].reshape(LEVEL * rows, size), sz[k])
        for q in range(LEVEL):
            piece = part[q * rows : (q + 1) * rows]
            usum[q] = piece if k == 0 else usum[q] + piece

    place = pl.multiple_of(zed * width, width)
    def along(k):
        part = sz.at[k, pl.ds(place, width), :]

        def body(d, carry):
            remote(part, part, z_send, z_recv.at[k], on_z(d)).start()
            return carry

        lax.fori_loop(1, nz, body, 0)

    solved = None
    for k in range(ticks):
        gather(a1, k, acc[k], a1_send, a1_recv)
        if k > 0:
            along(k - 1)
            for later in range(k + 1, ticks):
                update_row(k - 1, later, solved)
        if k == 1:
            pass_on()
        waiting = whole(a1, k, a1_recv)
        gather(a2, k, twice(nt_dot(waiting, dinv[k])), a2_send, a2_recv)
        if k >= 2:
            final(k - 2)
        solved = whole(a2, k, a2_recv)
        sz[k, pl.ds(place, width), :] = solved
        if k + 1 < ticks:
            update_row(k, k + 1, solved)
    along(ticks - 1)

    for k in range(max(ticks - 2, 0), ticks):
        final(k)

    def give(d, carry):
        remote(
            usum.at[lax.rem(cls + d, LEVEL)], ub.at[cls], u_send, u_recv, on_level(d)
        ).start()
        return carry

    lax.fori_loop(1, LEVEL, give, 0)
    ub[cls] = usum[cls]
    wait_for(ub.at[pl.ds(0, LEVEL - 1)], u_recv)
    for q in range(LEVEL):
        cut = slice(q * LANES, (q + 1) * LANES)
        out_ref[:, cut] = jnp.where(zed == 0, ub[q], pend[:, cut] - ub[q])

    wait_for(recv1, rs_send)
    wait_for(ub.at[pl.ds(0, LEVEL - 1)], u_send)
    wait_for(pin.at[pl.ds(0, LEVEL - 1)], sb_send)
    for _ in range(3):
        wait_for(wsrc, wl_send)
    for k in range(ticks):
        wait_for(a1.at[k, pl.ds(0, ncol - 1)], a1_send.at[k])
        wait_for(a2.at[k, pl.ds(0, ncol - 1)], a2_send.at[k])
        wait_for(sz.at[k, pl.ds(0, (nz - 1) * width)], z_send)

    @pl.when(zed == 0)
    def _():
        wait_for(pt.at[:, pl.ds(0, nz - 1)], sa_send)

    for j in range(LEVEL - 1):

        @pl.when((j < cls) & upward)
        def _():
            wait_for(wc.at[mine, j], wr_send)

        @pl.when((j < cls) & downward & (nz > 2))
        def _():
            wait_for(wc.at[mine, j], wr_send)

        @pl.when(j < cls)
        def _():
            wait_for(wc.at[pl.ds(0, LEVEL - 1), j], wc_send)


def per_device(right_side, prior_panel, prior_solved, window_panel, diag_inverse):
    rows, columns = right_side.shape[2:]
    size = prior_panel.shape[4]
    ticks = window_panel.shape[2]
    ncol = lax.axis_size("col")
    nz = lax.axis_size("row") // LEVEL
    width = LANES // nz
    dma = pltpu.SemaphoreType.DMA
    vmem = pltpu.VMEM
    out = pl.pallas_call(
        functools.partial(kernel, nz, ncol),
        out_shape=jax.ShapeDtypeStruct((rows, columns), F32),
        in_specs=[pl.BlockSpec(memory_space=pl.ANY)] * 5,
        out_specs=pl.BlockSpec(memory_space=pltpu.VMEM),
        scratch_shapes=[
            vmem((rows, columns), F32),
            vmem((size, size), BF16),
            vmem((size, columns), BF16),
            vmem((ticks, rows, size), BF16),
            vmem((ticks, rows, size), BF16),
            vmem((ncol, rows, columns), BF16),
            vmem((ncol - 1, rows, columns), BF16),
            vmem((rows, columns), F32),
            vmem((LEVEL, nz, width, LANES), BF16),
            vmem((LEVEL, width, LANES), BF16),
            vmem((LEVEL, width, LANES), BF16),
            vmem((ticks, width, LANES), F32),
            vmem((ticks, ncol, width, LANES), BF16),
            vmem((ticks, ncol, width, LANES), BF16),
            vmem((ticks, LANES, size), BF16),
            vmem((ticks, rows, size), BF16),
            vmem((ticks, LEVEL, rows, size), BF16),
            vmem((LEVEL - 1, LEVEL - 1, rows, size), BF16),
            vmem((LEVEL, rows, LANES), F32),
            vmem((LEVEL, rows, LANES), F32),
            dma((5,)),
            dma,
            dma,
            dma,
            dma,
            dma,
            dma,
            dma,
            dma((LEVEL - 1,)),
            dma,
            dma((LEVEL - 1, LEVEL - 1)),
            dma,
            dma((3,)),
            dma((ticks,)),
            dma((ticks,)),
            dma((ticks,)),
            dma((ticks,)),
            dma,
            dma((ticks,)),
            dma,
            dma,
        ],
        compiler_params=pltpu.CompilerParams(
            collective_id=0,
            has_side_effects=True,
            vmem_limit_bytes=60 * 1024 * 1024,
        ),
    )(
        right_side.reshape(rows, columns),
        prior_panel.reshape(size, size),
        prior_solved.reshape(size, columns),
        window_panel.reshape(ticks, rows, size),
        diag_inverse,
    )
    return out.reshape(right_side.shape)


def solution(mesh):
    return jax.shard_map(
        per_device,
        mesh=mesh,
        in_specs=(
            P(None, "row", "col", None),
            P(None, "row", None, "col", None, None),
            P(None, "col", None, None),
            P(None, "row", None, "col", None),
            P(None, "col", None),
        ),
        out_specs=P(None, "row", "col", None),
        check_vma=False,
    )
```

```python
import functools

import jax
import jax.numpy as jnp
from jax import lax
from jax.experimental import pallas as pl
from jax.experimental.pallas import tpu as pltpu
from jax.sharding import PartitionSpec as P

MESH = pl.DeviceIdType.MESH
F32 = jnp.float32
BF16 = jnp.bfloat16
LEVEL = 4
LANES = 128


def nt_dot(a, b):
    return lax.dot_general(
        a, b, (((1,), (1,)), ((), ())), preferred_element_type=F32
    )


def kernel(
    nz,
    ncol,
    rhs_h,
    panel_h,
    prior_h,
    win_h,
    dinv_h,
    out_ref,
    rhs,
    panel,
    prior,
    win,
    dinv,
    sendx,
    sendy,
    own,
    recvx,
    recvy,
    pend,
    pt,
    sca,
    pin,
    acc,
    turn,
    sz,
    wsrc,
    wl,
    wc,
    ybuf,
    tt,
    usum,
    ub,
    load_sem,
    x_send,
    x_recv,
    rs_send,
    rs_recv,
    sa_send,
    sa_recv,
    sb_send,
    sb_recv,
    wr_send,
    wr_recv,
    wc_send,
    wc_recv,
    wl_send,
    wl_recv,
    y_send,
    y_recv,
    tz_send,
    tz_recv,
    ts_send,
    ts_recv,
    t_send,
    t_recv,
    z_send,
    z_recv,
    u_send,
    u_recv,
):
    row = lax.axis_index("row")
    col = lax.axis_index("col")
    zed = row // LEVEL
    cls = row % LEVEL
    ticks, rows, size = win.shape
    width = pin.shape[1]
    columns = rhs.shape[1]
    near = ncol // 2
    half_at = col // near
    lane_at = col % near
    parity = col % 2

    loads = [
        pltpu.make_async_copy(src, dst, load_sem.at[i])
        for i, (src, dst) in enumerate(
            ((prior_h, prior), (panel_h, panel), (dinv_h, dinv), (win_h, win), (rhs_h, rhs))
        )
    ]
    for load in loads:
        load.start()

    far = sorted(
        ((dx, dy) for dx in range(2) for dy in range(near) if dx or dy),
        key=lambda p: -(2 * p[0] + min(p[1], near - p[1])),
    )

    def on_col(dx, dy):
        return (row, lax.rem(half_at + dx, 2) * near + lax.rem(lane_at + dy, near))

    def on_z(d):
        return (lax.rem(zed + d, nz) * LEVEL + cls, col)

    along_z = sorted(range(1, nz), key=lambda d: -min(d, nz - d))

    def on_level(d):
        return (zed * LEVEL + lax.rem(cls + d, LEVEL), col)

    def remote(src, dst, send, recv, device):
        return pltpu.make_async_remote_copy(
            src_ref=src,
            dst_ref=dst,
            send_sem=send,
            recv_sem=recv,
            device_id=device,
            device_id_type=MESH,
        )

    def wait_for(ref, sem):
        pltpu.make_async_copy(ref, ref, sem).wait()

    barrier = pltpu.get_barrier_semaphore()
    friends = [on_col(dx, dy) for dx, dy in far]
    friends += [on_z(d) for d in range(1, nz)] + [on_level(d) for d in range(1, LEVEL)]
    for friend in friends:
        pl.semaphore_signal(barrier, inc=1, device_id=friend, device_id_type=MESH)

    loads[0].wait()
    loads[1].wait()
    per_block = min(4, near)

    def product(at, out):
        def body(i, carry):
            start = pl.multiple_of((at * near + i * per_block) * rows, per_block * rows)
            part = jnp.dot(
                panel[pl.ds(start, per_block * rows), :],
                prior[...],
                preferred_element_type=F32,
            ).astype(out.dtype)
            for t in range(per_block):
                out[i * per_block + t] = part[t * rows : (t + 1) * rows]
            return carry

        lax.fori_loop(0, near // per_block, body, 0)

    order = sorted(range(near), key=lambda d: -min(d, near - d))
    product(1 - half_at, sendx)
    pl.semaphore_wait(barrier, len(friends))
    for i, dy in enumerate(order):
        to = lax.rem(lane_at + dy, near)
        remote(sendx.at[to], recvx.at[to], x_send, x_recv.at[i], on_col(1, 0)).start()

    loads[2].wait()
    loads[3].wait()
    active = cls >= 1
    mine = jnp.maximum(cls - 1, 0)

    def set_out(j):
        wc[mine, j] = win[j]
        for d in along_z:
            block = wc.at[mine, j]
            remote(block, block, wr_send, wr_recv.at[j], on_z(d)).start()

    @pl.when(active & (zed == 0))
    def _():
        set_out(mine)

    group = nz - 1 - zed
    lowest = group * (size // nz) // rows
    tile = pl.ds(pl.multiple_of(group * LANES, LANES), LANES)

    @pl.when(active & (col >= lowest))
    def _():
        ybuf[col] = dinv[mine, :, tile]
        for dx, dy in far:
            remote(
                ybuf.at[col], ybuf.at[col], y_send, y_recv.at[col], on_col(dx, dy)
            ).start()

    product(half_at, own)

    @pl.when(active)
    def _():
        @pl.when(zed > 0)
        def _():
            wait_for(wc.at[mine, mine], wr_recv.at[mine])

        for c in range(ncol):

            @pl.when((c >= lowest) & (col != c))
            def _():
                wait_for(ybuf.at[c], y_recv.at[c])

            @pl.when(c < lowest)
            def _():
                ybuf[c] = jnp.zeros((rows, LANES), BF16)

        tt[mine, group] = jnp.dot(
            wc[mine, mine], ybuf[...].reshape(size, LANES), preferred_element_type=F32
        ).astype(BF16)
        for d in along_z:
            part = tt.at[mine, group]
            remote(part, part, tz_send, tz_recv, on_z(d)).start()

    for i, dy in enumerate(order):
        to = lax.rem(lane_at + dy, near)
        wait_for(recvx.at[to], x_recv.at[i])
        both = own[to] + recvx[to].astype(F32)
        if dy == 0:
            own[to] = both
        else:
            sendy[to] = both.astype(BF16)
            remote(
                sendy.at[to], recvy.at[dy - 1], rs_send, rs_recv, on_col(0, dy)
            ).start()

    beyond = lax.rem(cls + 2, LEVEL)
    twin = cls + 1 - 2 * lax.rem(cls, 2)
    on_beyond = (zed * LEVEL + beyond, col)
    on_twin = (zed * LEVEL + twin, col)

    def exchange():
        @pl.when(zed == 0)
        def _():
            picks = (
                lax.broadcasted_iota(jnp.int32, (rows, size), 1)
                == lax.broadcasted_iota(jnp.int32, (rows, size), 0) + col * rows
            )
            for k in range(ticks):
                wsrc[k] = jnp.where(picks & (cls == k), 1.0, 0.0).astype(BF16)

        @pl.when(zed > 0)
        def _():
            wsrc[...] = win[...]

        remote(wsrc, wl.at[:, cls], wl_send, wl_recv.at[0], on_beyond).start()
        remote(wsrc, wl.at[:, cls], wl_send, wl_recv.at[1], on_twin).start()
        wl[:, cls] = wsrc[...]

    def pass_on():
        there = wl.at[:, beyond]
        wait_for(there, wl_recv.at[0])
        remote(there, there, wl_send, wl_recv.at[2], on_twin).start()

    exchange()

    def settle():
        wait_for(recvy, rs_recv)
        total = own[lane_at]
        for d in range(near - 1):
            total = total + recvy[d].astype(F32)
        pend[...] = rhs[...] - total

    loads[4].wait()

    @pl.when(zed == 0)
    def _():
        settle()
        value = pend[...]
        for q in range(LEVEL):
            part = jnp.concatenate(
                [value[:, q * LANES : (q + 1) * LANES]] * 2, axis=0
            ).T.astype(BF16)
            for t in range(nz):
                pt[q, t] = part[t * width : (t + 1) * width]
        for d in along_z:
            remote(pt.at[:, d], sca, sa_send, sa_recv, on_z(d)).start()
        sca[...] = pt[:, 0]

    for j in range(LEVEL - 2):

        @pl.when((j < cls - 1) & (zed == 0))
        def _():
            set_out(j)

    def share_window():
        for j in range(LEVEL - 2):

            @pl.when(j < cls - 1)
            def _():
                block = wc.at[mine, j]

                @pl.when(zed > 0)
                def _():
                    wait_for(block, wr_recv.at[j])

                for d in range(1, LEVEL):
                    remote(
                        block, block, wc_send, wc_recv.at[mine, j], on_level(d)
                    ).start()

    @pl.when(zed > 0)
    def _():
        wait_for(sca, sa_recv)

    for d in range(1, LEVEL):
        to = lax.rem(cls + d, LEVEL)
        remote(sca.at[to], pin.at[cls], sb_send, sb_recv, on_level(d)).start()
    pin[cls] = sca[cls]

    @pl.when(active)
    def _():
        wait_for(tt.at[mine, pl.ds(0, nz - 1)], tz_recv)
        for d in range(1, LEVEL):
            part = tt.at[mine]
            remote(part, part, ts_send, ts_recv.at[mine], on_level(d)).start()

    wait_for(pin.at[pl.ds(0, LEVEL - 1)], sb_recv)
    for k in range(ticks):
        acc[k] = pin[k].astype(F32)

    lane = lax.broadcasted_iota(jnp.int32, (width, LANES), 1)
    kept = (lane >= parity * rows) & (lane < parity * rows + rows)

    def twice(value):
        return jnp.concatenate([value, value], axis=1)

    def put(n, slot, value):
        turn[n, col, slot] = jnp.where(kept, value, 0.0).astype(BF16)

    def slots(n):
        return pl.ds(0 if n < ticks else 1, 2 if 0 < n < ticks else 1)

    def gather(n):
        part = turn.at[n, col, slots(n)]
        for dx, dy in far:
            remote(part, part, t_send.at[n], t_recv.at[n], on_col(dx, dy)).start()

    def whole(n, slot):
        return jnp.concatenate(
            [turn[n, 2 * p, slot] + turn[n, 2 * p + 1, slot] for p in range(near)],
            axis=1,
        )

    def window_term(later, k, solved):
        @pl.when(cls != later)
        def _():
            wait_for(wc.at[later - 1, k], wc_recv.at[later - 1, k])

        return twice(nt_dot(solved, wc[later - 1, k]))

    def fold_term(n, waiting):
        @pl.when(cls != n + 1)
        def _():
            wait_for(tt.at[n], ts_recv.at[n])

        fold = jnp.concatenate([tt[n, g] for g in range(nz)], axis=1)
        return twice(nt_dot(waiting, fold))

    place = pl.multiple_of(zed * width, width)

    def along(k):
        part = sz.at[k, pl.ds(place, width), :]
        for d in along_z:
            remote(part, part, z_send, z_recv.at[k], on_z(d)).start()

    def final(k):
        if k == 0:
            for way in range(1, 3):
                wait_for(wsrc, wl_recv.at[way])
        wait_for(sz.at[k, pl.ds(0, (nz - 1) * width)], z_recv.at[k])
        part = nt_dot(wl[k].reshape(LEVEL * rows, size), sz[k])
        for q in range(LEVEL):
            piece = part[q * rows : (q + 1) * rows]
            usum[q] = piece if k == 0 else usum[q] + piece

    put(0, 0, acc[0])
    gather(0)
    for n in range(ticks + 1):
        wait_for(turn.at[n, pl.ds(0, ncol - 1), slots(n)], t_recv.at[n])
        solved = whole(n, 1) if n > 0 else None
        if n < ticks:
            waiting = whole(n, 0)
            put(n + 1, 1, twice(nt_dot(waiting, dinv[n])))
            if n + 1 < ticks:
                value = acc[n + 1] - fold_term(n, waiting)
                if n > 0:
                    value = value - window_term(n + 1, n - 1, solved)
                put(n + 1, 0, value)
            gather(n + 1)
        if n > 0:
            sz[n - 1, pl.ds(place, width), :] = solved
            along(n - 1)
            for later in range(n + 2, ticks):
                acc[later] = acc[later] - window_term(later, n - 1, solved)
        if n == 0:
            share_window()
        if n == 1:
            pass_on()

            @pl.when(zed > 0)
            def _():
                settle()

        if n >= 2:
            final(n - 2)
    final(ticks - 1)

    for d in range(1, LEVEL):
        to = lax.rem(cls + d, LEVEL)
        remote(usum.at[to], ub.at[cls], u_send, u_recv, on_level(d)).start()
    ub[cls] = usum[cls]
    wait_for(ub.at[pl.ds(0, LEVEL - 1)], u_recv)
    for q in range(LEVEL):
        cut = slice(q * LANES, (q + 1) * LANES)
        out_ref[:, cut] = jnp.where(zed == 0, ub[q], pend[:, cut] - ub[q])

    wait_for(recvx, x_send)
    wait_for(recvy, rs_send)
    wait_for(ub.at[pl.ds(0, LEVEL - 1)], u_send)
    wait_for(pin.at[pl.ds(0, LEVEL - 1)], sb_send)
    for _ in range(3):
        wait_for(wsrc, wl_send)
    for n in range(ticks + 1):
        wait_for(turn.at[n, pl.ds(0, ncol - 1), slots(n)], t_send.at[n])
    for k in range(ticks):
        wait_for(sz.at[k, pl.ds(0, (nz - 1) * width)], z_send)

    @pl.when(zed == 0)
    def _():
        wait_for(pt.at[:, pl.ds(0, nz - 1)], sa_send)

    @pl.when(active & (col >= lowest))
    def _():
        wait_for(ybuf.at[pl.ds(0, ncol - 1)], y_send)

    @pl.when(active)
    def _():
        wait_for(tt.at[mine, pl.ds(0, nz - 1)], tz_send)
        for _ in range(LEVEL - 1):
            wait_for(tt.at[mine], ts_send)

    for j in range(LEVEL - 1):

        @pl.when((j < cls) & (zed == 0))
        def _():
            for _ in along_z:
                wait_for(wc.at[mine, j], wr_send)

        @pl.when(j < cls - 1)
        def _():
            wait_for(wc.at[pl.ds(0, LEVEL - 1), j], wc_send)


def per_device(right_side, prior_panel, prior_solved, window_panel, diag_inverse):
    rows, columns = right_side.shape[2:]
    size = prior_panel.shape[4]
    ticks = window_panel.shape[2]
    ncol = lax.axis_size("col")
    nz = lax.axis_size("row") // LEVEL
    width = LANES // nz
    near = ncol // 2
    dma = pltpu.SemaphoreType.DMA
    vmem = pltpu.VMEM
    out = pl.pallas_call(
        functools.partial(kernel, nz, ncol),
        out_shape=jax.ShapeDtypeStruct((rows, columns), F32),
        in_specs=[pl.BlockSpec(memory_space=pl.ANY)] * 5,
        out_specs=pl.BlockSpec(memory_space=pltpu.VMEM),
        scratch_shapes=[
            vmem((rows, columns), F32),
            vmem((size, size), BF16),
            vmem((size, columns), BF16),
            vmem((ticks, rows, size), BF16),
            vmem((ticks, rows, size), BF16),
            vmem((near, rows, columns), BF16),
            vmem((near, rows, columns), BF16),
            vmem((near, rows, columns), F32),
            vmem((near, rows, columns), BF16),
            vmem((near - 1, rows, columns), BF16),
            vmem((rows, columns), F32),
            vmem((LEVEL, nz, width, LANES), BF16),
            vmem((LEVEL, width, LANES), BF16),
            vmem((LEVEL, width, LANES), BF16),
            vmem((ticks, width, LANES), F32),
            vmem((ticks + 1, ncol, 2, width, LANES), BF16),
            vmem((ticks, LANES, size), BF16),
            vmem((ticks, rows, size), BF16),
            vmem((ticks, LEVEL, rows, size), BF16),
            vmem((LEVEL - 1, LEVEL - 1, rows, size), BF16),
            vmem((ncol, rows, LANES), BF16),
            vmem((LEVEL - 1, nz, rows, LANES), BF16),
            vmem((LEVEL, rows, LANES), F32),
            vmem((LEVEL, rows, LANES), F32),
            dma((5,)),
            dma,
            dma((near,)),
            dma,
            dma,
            dma,
            dma,
            dma,
            dma,
            dma,
            dma((LEVEL - 1,)),
            dma,
            dma((LEVEL - 1, LEVEL - 1)),
            dma,
            dma((3,)),
            dma,
            dma((ncol,)),
            dma,
            dma,
            dma,
            dma((LEVEL - 1,)),
            dma((ticks + 1,)),
            dma((ticks + 1,)),
            dma,
            dma((ticks,)),
            dma,
            dma,
        ],
        compiler_params=pltpu.CompilerParams(
            collective_id=0,
            has_side_effects=True,
            vmem_limit_bytes=60 * 1024 * 1024,
        ),
    )(
        right_side.reshape(rows, columns),
        prior_panel.reshape(size, size),
        prior_solved.reshape(size, columns),
        window_panel.reshape(ticks, rows, size),
        diag_inverse,
    )
    return out.reshape(right_side.shape)


def solution(mesh):
    return jax.shard_map(
        per_device,
        mesh=mesh,
        in_specs=(
            P(None, "row", "col", None),
            P(None, "row", None, "col", None, None),
            P(None, "col", None, None),
            P(None, "row", None, "col", None),
            P(None, "col", None),
        ),
        out_specs=P(None, "row", "col", None),
        check_vma=False,
    )
```

```python
import functools

import jax
import jax.numpy as jnp
from jax import lax
from jax.experimental import pallas as pl
from jax.experimental.pallas import tpu as pltpu
from jax.sharding import PartitionSpec as P

MESH = pl.DeviceIdType.MESH
F32 = jnp.float32
BF16 = jnp.bfloat16
LEVEL = 4
LANES = 128


def nt_dot(a, b):
    return lax.dot_general(
        a, b, (((1,), (1,)), ((), ())), preferred_element_type=F32
    )


def kernel(
    nz,
    ncol,
    rhs_h,
    panel_h,
    prior_h,
    win_h,
    dinv_h,
    out_ref,
    rhs,
    panel,
    prior,
    win,
    dinv,
    sendx,
    sendy,
    own,
    recvx,
    recvy,
    pend,
    pt,
    sca,
    pin,
    acc,
    turn,
    sz,
    wl,
    wc,
    ybuf,
    tt,
    usum,
    ub,
    load_sem,
    x_send,
    x_recv,
    rs_send,
    rs_recv,
    sa_send,
    sa_recv,
    sb_send,
    sb_recv,
    wr_send,
    wr_recv,
    wh_send,
    wh_recv,
    wo_send,
    wo_recv,
    wc_send,
    wc_recv,
    wl_send,
    wl_recv,
    y_send,
    y_recv,
    tz_send,
    tz_recv,
    ts_send,
    ts_recv,
    t_send,
    t_recv,
    z_send,
    z_recv,
    u_send,
    u_recv,
):
    row = lax.axis_index("row")
    col = lax.axis_index("col")
    zed = row // LEVEL
    cls = row % LEVEL
    ticks, rows, size = win.shape
    width = pin.shape[1]
    columns = rhs.shape[1]
    near = ncol // 2
    half_at = col // near
    lane_at = col % near
    parity = col % 2

    loads = [
        pltpu.make_async_copy(src, dst, load_sem.at[i])
        for i, (src, dst) in enumerate(
            ((prior_h, prior), (panel_h, panel), (dinv_h, dinv), (win_h, win), (rhs_h, rhs))
        )
    ]
    for load in loads:
        load.start()

    far = sorted(
        ((dx, dy) for dx in range(2) for dy in range(near) if dx or dy),
        key=lambda p: -(2 * p[0] + min(p[1], near - p[1])),
    )

    def on_col(dx, dy):
        return (row, lax.rem(half_at + dx, 2) * near + lax.rem(lane_at + dy, near))

    def on_z(d):
        return (lax.rem(zed + d, nz) * LEVEL + cls, col)

    along_z = sorted(range(1, nz), key=lambda d: -min(d, nz - d))

    def on_level(d):
        return (zed * LEVEL + lax.rem(cls + d, LEVEL), col)

    def remote(src, dst, send, recv, device):
        return pltpu.make_async_remote_copy(
            src_ref=src,
            dst_ref=dst,
            send_sem=send,
            recv_sem=recv,
            device_id=device,
            device_id_type=MESH,
        )

    def wait_for(ref, sem):
        pltpu.make_async_copy(ref, ref, sem).wait()

    barrier = pltpu.get_barrier_semaphore()
    friends = [on_col(dx, dy) for dx, dy in far]
    friends += [on_z(d) for d in range(1, nz)] + [on_level(d) for d in range(1, LEVEL)]
    for friend in friends:
        pl.semaphore_signal(barrier, inc=1, device_id=friend, device_id_type=MESH)

    loads[0].wait()
    loads[1].wait()
    per_block = min(4, near)

    def product(at, out):
        def body(i, carry):
            start = pl.multiple_of((at * near + i * per_block) * rows, per_block * rows)
            part = jnp.dot(
                panel[pl.ds(start, per_block * rows), :],
                prior[...],
                preferred_element_type=F32,
            ).astype(out.dtype)
            for t in range(per_block):
                out[i * per_block + t] = part[t * rows : (t + 1) * rows]
            return carry

        lax.fori_loop(0, near // per_block, body, 0)

    order = sorted(range(near), key=lambda d: -min(d, near - d))
    product(1 - half_at, sendx)
    loads[2].wait()
    loads[3].wait()
    active = cls >= 1
    mine = jnp.maximum(cls - 1, 0)
    carrier = cls < LEVEL - 1
    carried = wc.at[jnp.where(cls == 2, 1, 2), jnp.where(cls == 1, 1, 0)]
    begin = near // 2
    trunk = sorted(range(2, nz, 2), key=lambda d: -min(d, nz - d)) or [1]
    branch = (zed % 4 == 2) if nz > 2 else (zed < 0)

    def set_out(i, block, send, recv):
        if i in range(len(trunk)):
            remote(block, block, send, recv, on_z(trunk[i])).start()

    def branch_out(block, send, recv):
        for d in (1, nz - 1):
            remote(block, block, send, recv, on_z(d)).start()

    group = nz - 1 - zed
    lowest = group * (size // nz) // rows
    tile = pl.ds(pl.multiple_of(group * LANES, LANES), LANES)
    pl.semaphore_wait(barrier, len(friends))

    @pl.when(active & (col >= lowest))
    def _():
        ybuf[col] = dinv[mine, :, tile]
        for dx, dy in far:
            remote(
                ybuf.at[col], ybuf.at[col], y_send, y_recv.at[col], on_col(dx, dy)
            ).start()

    def send_x(some):
        for i in some:
            to = lax.rem(lane_at + order[i], near)
            remote(sendx.at[to], recvx.at[to], x_send, x_recv.at[i], on_col(1, 0)).start()

    def first_out(who):
        @pl.when((zed == 0) & who)
        def _():
            wc[mine, mine] = win[mine]
            for i in range(len(trunk)):
                set_out(i, wc.at[mine, mine], wr_send, wr_recv)

    first_out(cls == 1)
    send_x(range(begin))

    @pl.when(zed == 0)
    def _():
        send_x(range(begin, near))

    first_out(cls > 1)

    @pl.when((zed == 0) & (cls == LEVEL - 1))
    def _():
        for j in range(2):
            remote(win.at[j], wc.at[2, j], wh_send, wh_recv, (j, col)).start()

    product(half_at, own)

    @pl.when(active & (zed > 0))
    def _():
        wait_for(wc.at[mine, mine], wr_recv)

        @pl.when(branch)
        def _():
            branch_out(wc.at[mine, mine], wr_send, wr_recv)

    @pl.when(zed > 0)
    def _():
        send_x(range(begin, near))

    @pl.when(active)
    def _():
        for c in range(ncol):

            @pl.when((c >= lowest) & (col != c))
            def _():
                wait_for(ybuf.at[c], y_recv.at[c])

            @pl.when(c < lowest)
            def _():
                ybuf[c] = jnp.zeros((rows, LANES), BF16)

        tt[mine, group] = jnp.dot(
            wc[mine, mine], ybuf[...].reshape(size, LANES), preferred_element_type=F32
        ).astype(BF16)
        for d in along_z:
            part = tt.at[mine, group]
            remote(part, part, tz_send, tz_recv, on_z(d)).start()

    beyond = lax.rem(cls + 2, LEVEL)
    twin = cls + 1 - 2 * lax.rem(cls, 2)
    on_beyond = (zed * LEVEL + beyond, col)
    on_twin = (zed * LEVEL + twin, col)
    pieces = 2 * ticks // near

    for i, dy in enumerate(order):
        to = lax.rem(lane_at + dy, near)
        wait_for(recvx.at[to], x_recv.at[i])
        both = own[to] + recvx[to].astype(F32)
        if dy == 0:
            own[to] = both
        else:
            sendy[to] = both.astype(BF16)
            remote(
                sendy.at[to], recvy.at[dy - 1], rs_send, rs_recv, on_col(0, dy)
            ).start()

        @pl.when(zed > 0)
        def _():
            for piece in range(i * pieces, (i + 1) * pieces):
                k, side = piece // 2, pl.ds(piece % 2 * (rows // 2), rows // 2)
                remote(
                    win.at[k, side], wl.at[k, cls, side], wl_send, wl_recv.at[0], on_beyond
                ).start()

        if i == begin - 1:

            @pl.when((zed == 0) & (cls == 2))
            def _():
                wc[1, 0] = win[0]

            @pl.when((zed == 0) & (cls < 2))
            def _():
                wait_for(carried, wh_recv)

        @pl.when((zed == 0) & carrier)
        def _():
            set_out(i + 1 - begin, carried, wo_send, wo_recv)

    @pl.when(zed > 0)
    def _():
        remote(win, wl.at[:, cls], wl_send, wl_recv.at[1], on_twin).start()

    def pass_on():
        @pl.when(zed == 0)
        def _():
            picks = (
                lax.broadcasted_iota(jnp.int32, (rows, size), 1)
                == lax.broadcasted_iota(jnp.int32, (rows, size), 0) + col * rows
            )
            for k in range(ticks):
                for q in range(LEVEL):
                    wl[k, q] = jnp.where(picks & (k == q), 1.0, 0.0).astype(BF16)

        @pl.when(zed > 0)
        def _():
            wl[:, cls] = win[...]
            there = wl.at[:, beyond]
            wait_for(there, wl_recv.at[0])
            remote(there, there, wl_send, wl_recv.at[2], on_twin).start()

    def settle():
        wait_for(recvy, rs_recv)
        total = own[lane_at]
        for d in range(near - 1):
            total = total + recvy[d].astype(F32)
        pend[...] = rhs[...] - total

    loads[4].wait()

    @pl.when(zed == 0)
    def _():
        settle()
        value = pend[...]
        for q in range(LEVEL):
            part = jnp.concatenate(
                [value[:, q * LANES : (q + 1) * LANES]] * 2, axis=0
            ).T.astype(BF16)
            for t in range(nz):
                pt[q, t] = part[t * width : (t + 1) * width]
        for d in along_z:
            remote(pt.at[:, d], sca, sa_send, sa_recv, on_z(d)).start()
        sca[...] = pt[:, 0]

    @pl.when((zed > 0) & branch & carrier)
    def _():
        wait_for(carried, wo_recv)
        branch_out(carried, wo_send, wo_recv)

    def deal(who):
        @pl.when(who & (zed > 0))
        def _():
            wait_for(sca, sa_recv)

        @pl.when(who)
        def _():
            for d in range(1, LEVEL):
                to = lax.rem(cls + d, LEVEL)
                remote(
                    sca.at[to], pin.at[cls], sb_send, sb_recv.at[cls], on_level(d)
                ).start()
            pin[cls] = sca[cls]

    def take(k):
        @pl.when(cls != k)
        def _():
            wait_for(pin.at[k], sb_recv.at[k])

        return pin[k].astype(F32)

    deal(cls == 0)

    lane = lax.broadcasted_iota(jnp.int32, (width, LANES), 1)
    kept = (lane >= parity * rows) & (lane < parity * rows + rows)

    def twice(value):
        return jnp.concatenate([value, value], axis=1)

    def put(n, slot, value):
        turn[n, col, slot] = jnp.where(kept, value, 0.0).astype(BF16)

    def slots(n):
        return pl.ds(0 if n < ticks else 1, 2 if 0 < n < ticks else 1)

    def gather(n):
        part = turn.at[n, col, slots(n)]
        for dx, dy in far:
            remote(part, part, t_send.at[n], t_recv.at[n], on_col(dx, dy)).start()

    def whole(n, slot):
        return jnp.concatenate(
            [turn[n, 2 * p, slot] + turn[n, 2 * p + 1, slot] for p in range(near)],
            axis=1,
        )

    def window_term(later, k, solved):
        @pl.when(cls != (2 if later == 2 else k))
        def _():
            wait_for(wc.at[later - 1, k], wc_recv.at[later - 1, k])

        return twice(nt_dot(solved, wc[later - 1, k]))

    def fold_term(n, waiting):
        @pl.when(cls != n + 1)
        def _():
            wait_for(tt.at[n], ts_recv.at[n])

        fold = jnp.concatenate([tt[n, g] for g in range(nz)], axis=1)
        return twice(nt_dot(waiting, fold))

    place = pl.multiple_of(zed * width, width)

    def along(k):
        part = sz.at[k, pl.ds(place, width), :]
        for d in along_z:
            remote(part, part, z_send, z_recv.at[k], on_z(d)).start()

    def final(k):
        if k == 0:

            @pl.when(zed > 0)
            def _():
                for way in range(1, 3):
                    wait_for(win, wl_recv.at[way])

        wait_for(sz.at[k, pl.ds(0, (nz - 1) * width)], z_recv.at[k])
        part = nt_dot(wl[k].reshape(LEVEL * rows, size), sz[k])
        for q in range(LEVEL):
            piece = part[q * rows : (q + 1) * rows]
            usum[q] = piece if k == 0 else usum[q] + piece

    def share_fold(who):
        @pl.when(who)
        def _():
            wait_for(tt.at[mine, pl.ds(0, nz - 1)], tz_recv)
            for d in range(1, LEVEL):
                part = tt.at[mine]
                remote(part, part, ts_send, ts_recv.at[mine], on_level(d)).start()

    def share_window(who):
        @pl.when(who)
        def _():
            @pl.when((zed > 0) & jnp.logical_not(branch))
            def _():
                wait_for(carried, wo_recv)

            at = jnp.where(cls == 2, 1, 2), jnp.where(cls == 1, 1, 0)
            for d in range(1, LEVEL):
                remote(carried, carried, wc_send, wc_recv.at[at], on_level(d)).start()

    put(0, 0, take(0))
    gather(0)
    deal(cls > 0)
    share_fold((cls == 1) | (cls == 2))
    share_window((cls == 0) | (cls == 2))
    for n in range(ticks + 1):
        wait_for(turn.at[n, pl.ds(0, ncol - 1), slots(n)], t_recv.at[n])
        if n == 0:
            for k in range(1, ticks):
                acc[k] = take(k)
        solved = whole(n, 1) if n > 0 else None
        if n < ticks:
            waiting = whole(n, 0)
            put(n + 1, 1, twice(nt_dot(waiting, dinv[n])))
            if n + 1 < ticks:
                value = acc[n + 1] - fold_term(n, waiting)
                if n > 0:
                    value = value - window_term(n + 1, n - 1, solved)
                put(n + 1, 0, value)
            gather(n + 1)
        if n > 0:
            sz[n - 1, pl.ds(place, width), :] = solved
            along(n - 1)
            for later in range(n + 2, ticks):
                acc[later] = acc[later] - window_term(later, n - 1, solved)
        if n == 0:
            share_fold(cls == 3)
            share_window(cls == 1)
        if n == 1:
            pass_on()

            @pl.when(zed > 0)
            def _():
                settle()

        if n >= 2:
            final(n - 2)
    final(ticks - 1)

    for d in range(1, LEVEL):
        to = lax.rem(cls + d, LEVEL)
        remote(usum.at[to], ub.at[cls], u_send, u_recv, on_level(d)).start()
    ub[cls] = usum[cls]
    wait_for(ub.at[pl.ds(0, LEVEL - 1)], u_recv)
    for q in range(LEVEL):
        cut = slice(q * LANES, (q + 1) * LANES)
        out_ref[:, cut] = jnp.where(zed == 0, ub[q], pend[:, cut] - ub[q])

    wait_for(recvx, x_send)
    wait_for(recvy, rs_send)
    wait_for(ub.at[pl.ds(0, LEVEL - 1)], u_send)
    wait_for(pin.at[pl.ds(0, LEVEL - 1)], sb_send)

    @pl.when(zed > 0)
    def _():
        for _ in range(3):
            wait_for(win, wl_send)

    for n in range(ticks + 1):
        wait_for(turn.at[n, pl.ds(0, ncol - 1), slots(n)], t_send.at[n])
    for k in range(ticks):
        wait_for(sz.at[k, pl.ds(0, (nz - 1) * width)], z_send)

    @pl.when(zed == 0)
    def _():
        wait_for(pt.at[:, pl.ds(0, nz - 1)], sa_send)

    @pl.when(active & (col >= lowest))
    def _():
        wait_for(ybuf.at[pl.ds(0, ncol - 1)], y_send)

    @pl.when(active)
    def _():
        wait_for(tt.at[mine, pl.ds(0, nz - 1)], tz_send)
        for _ in range(LEVEL - 1):
            wait_for(tt.at[mine], ts_send)

    @pl.when(active & (zed == 0))
    def _():
        for _ in trunk:
            wait_for(wc.at[mine, mine], wr_send)

    @pl.when(carrier & (zed == 0))
    def _():
        for _ in trunk:
            wait_for(carried, wo_send)

    @pl.when(active & branch)
    def _():
        for _ in range(2):
            wait_for(wc.at[mine, mine], wr_send)

    @pl.when(carrier & branch)
    def _():
        for _ in range(2):
            wait_for(carried, wo_send)

    @pl.when((zed == 0) & (cls == LEVEL - 1))
    def _():
        wait_for(wc.at[2, pl.ds(0, 2)], wh_send)

    @pl.when(carrier)
    def _():
        wait_for(wc.at[0], wc_send)


def per_device(right_side, prior_panel, prior_solved, window_panel, diag_inverse):
    rows, columns = right_side.shape[2:]
    size = prior_panel.shape[4]
    ticks = window_panel.shape[2]
    ncol = lax.axis_size("col")
    nz = lax.axis_size("row") // LEVEL
    width = LANES // nz
    near = ncol // 2
    dma = pltpu.SemaphoreType.DMA
    vmem = pltpu.VMEM
    out = pl.pallas_call(
        functools.partial(kernel, nz, ncol),
        out_shape=jax.ShapeDtypeStruct((rows, columns), F32),
        in_specs=[pl.BlockSpec(memory_space=pl.ANY)] * 5,
        out_specs=pl.BlockSpec(memory_space=pltpu.VMEM),
        scratch_shapes=[
            vmem((rows, columns), F32),
            vmem((size, size), BF16),
            vmem((size, columns), BF16),
            vmem((ticks, rows, size), BF16),
            vmem((ticks, rows, size), BF16),
            vmem((near, rows, columns), BF16),
            vmem((near, rows, columns), BF16),
            vmem((near, rows, columns), F32),
            vmem((near, rows, columns), BF16),
            vmem((near - 1, rows, columns), BF16),
            vmem((rows, columns), F32),
            vmem((LEVEL, nz, width, LANES), BF16),
            vmem((LEVEL, width, LANES), BF16),
            vmem((LEVEL, width, LANES), BF16),
            vmem((ticks, width, LANES), F32),
            vmem((ticks + 1, ncol, 2, width, LANES), BF16),
            vmem((ticks, LANES, size), BF16),
            vmem((ticks, LEVEL, rows, size), BF16),
            vmem((LEVEL - 1, LEVEL - 1, rows, size), BF16),
            vmem((ncol, rows, LANES), BF16),
            vmem((LEVEL - 1, nz, rows, LANES), BF16),
            vmem((LEVEL, rows, LANES), F32),
            vmem((LEVEL, rows, LANES), F32),
            dma((5,)),
            dma,
            dma((near,)),
            dma,
            dma,
            dma,
            dma,
            dma,
            dma((LEVEL,)),
            dma,
            dma,
            dma,
            dma,
            dma,
            dma,
            dma,
            dma((LEVEL - 1, LEVEL - 1)),
            dma,
            dma((3,)),
            dma,
            dma((ncol,)),
            dma,
            dma,
            dma,
            dma((LEVEL - 1,)),
            dma((ticks + 1,)),
            dma((ticks + 1,)),
            dma,
            dma((ticks,)),
            dma,
            dma,
        ],
        compiler_params=pltpu.CompilerParams(
            collective_id=0,
            has_side_effects=True,
            vmem_limit_bytes=60 * 1024 * 1024,
        ),
    )(
        right_side.reshape(rows, columns),
        prior_panel.reshape(size, size),
        prior_solved.reshape(size, columns),
        window_panel.reshape(ticks, rows, size),
        diag_inverse,
    )
    return out.reshape(right_side.shape)


def solution(mesh):
    return jax.shard_map(
        per_device,
        mesh=mesh,
        in_specs=(
            P(None, "row", "col", None),
            P(None, "row", None, "col", None, None),
            P(None, "col", None, None),
            P(None, "row", None, "col", None),
            P(None, "col", None),
        ),
        out_specs=P(None, "row", "col", None),
        check_vma=False,
    )
```

```python
import functools

import jax
import jax.numpy as jnp
from jax import lax
from jax.experimental import pallas as pl
from jax.experimental.pallas import tpu as pltpu
from jax.sharding import PartitionSpec as P

MESH = pl.DeviceIdType.MESH
F32 = jnp.float32
BF16 = jnp.bfloat16
LEVEL = 4
LANES = 128


def nt_dot(a, b):
    return lax.dot_general(
        a, b, (((1,), (1,)), ((), ())), preferred_element_type=F32
    )


def kernel(
    nz,
    ncol,
    rhs_h,
    panel_h,
    prior_h,
    win_h,
    dinv_h,
    out_ref,
    rhs,
    panel,
    prior,
    win,
    dinv,
    sendx,
    sendy,
    own,
    recvx,
    recvy,
    pend,
    pt,
    sca,
    pin,
    acc,
    turn,
    sz,
    wl,
    wc,
    ybuf,
    tt,
    usum,
    ub,
    load_sem,
    x_send,
    x_recv,
    rs_send,
    rs_recv,
    sa_send,
    sa_recv,
    sb_send,
    sb_recv,
    wr_send,
    wr_recv,
    wh_send,
    wh_recv,
    wo_send,
    wo_recv,
    wc_send,
    wc_recv,
    wl_send,
    wl_recv,
    y_send,
    y_recv,
    tz_send,
    tz_recv,
    ts_send,
    ts_recv,
    t_send,
    t_recv,
    z_send,
    z_recv,
    u_send,
    u_recv,
):
    row = lax.axis_index("row")
    col = lax.axis_index("col")
    zed = row // LEVEL
    cls = row % LEVEL
    ticks, rows, size = win.shape
    width = pin.shape[1]
    columns = rhs.shape[1]
    near = ncol // 2
    half_at = col // near
    lane_at = col % near
    parity = col % 2

    loads = [
        pltpu.make_async_copy(src, dst, load_sem.at[i])
        for i, (src, dst) in enumerate(
            ((prior_h, prior), (panel_h, panel), (dinv_h, dinv), (win_h, win), (rhs_h, rhs))
        )
    ]
    for load in loads:
        load.start()

    far = sorted(
        ((dx, dy) for dx in range(2) for dy in range(near) if dx or dy),
        key=lambda p: -(2 * p[0] + min(p[1], near - p[1])),
    )

    def on_col(dx, dy):
        return (row, lax.rem(half_at + dx, 2) * near + lax.rem(lane_at + dy, near))

    def on_z(d):
        return (lax.rem(zed + d, nz) * LEVEL + cls, col)

    along_z = sorted(range(1, nz), key=lambda d: -min(d, nz - d))

    def on_level(d):
        return (zed * LEVEL + lax.rem(cls + d, LEVEL), col)

    def remote(src, dst, send, recv, device):
        return pltpu.make_async_remote_copy(
            src_ref=src,
            dst_ref=dst,
            send_sem=send,
            recv_sem=recv,
            device_id=device,
            device_id_type=MESH,
        )

    def wait_for(ref, sem):
        pltpu.make_async_copy(ref, ref, sem).wait()

    barrier = pltpu.get_barrier_semaphore()
    friends = [(2 * dx + min(dy, near - dy), on_col(dx, dy)) for dx, dy in far]
    friends += [(min(d, nz - d), on_z(d)) for d in along_z]
    friends += [(1, on_level(d)) for d in range(1, LEVEL)]
    for _, friend in sorted(friends, key=lambda p: -p[0]):
        pl.semaphore_signal(barrier, inc=1, device_id=friend, device_id_type=MESH)

    loads[0].wait()
    loads[1].wait()
    per_block = min(4, near)

    def product(at, out):
        def body(i, carry):
            start = pl.multiple_of((at * near + i * per_block) * rows, per_block * rows)
            part = jnp.dot(
                panel[pl.ds(start, per_block * rows), :],
                prior[...],
                preferred_element_type=F32,
            ).astype(out.dtype)
            for t in range(per_block):
                out[i * per_block + t] = part[t * rows : (t + 1) * rows]
            return carry

        lax.fori_loop(0, near // per_block, body, 0)

    order = sorted(range(near), key=lambda d: -min(d, near - d))
    product(1 - half_at, sendx)
    loads[2].wait()
    loads[3].wait()
    active = cls >= 1
    mine = jnp.maximum(cls - 1, 0)
    carrier = cls < LEVEL - 1
    carried = wc.at[jnp.where(cls == 2, 1, 2), jnp.where(cls == 1, 1, 0)]
    begin = near // 2
    trunk = sorted(range(2, nz, 2), key=lambda d: -min(d, nz - d)) or [1]
    branch = (zed % 4 == 2) if nz > 2 else (zed < 0)

    def set_out(i, block, send, recv):
        if i in range(len(trunk)):
            remote(block, block, send, recv, on_z(trunk[i])).start()

    def branch_out(block, send, recv):
        for d in (1, nz - 1):
            remote(block, block, send, recv, on_z(d)).start()

    group = nz - 1 - zed
    lowest = group * (size // nz) // rows
    tile = pl.ds(pl.multiple_of(group * LANES, LANES), LANES)
    pl.semaphore_wait(barrier, len(friends))

    @pl.when(active & (col >= lowest))
    def _():
        ybuf[col] = dinv[mine, :, tile]
        for dx, dy in far:
            remote(
                ybuf.at[col], ybuf.at[col], y_send, y_recv.at[col], on_col(dx, dy)
            ).start()

    def send_x(some):
        for i in some:
            to = lax.rem(lane_at + order[i], near)
            remote(sendx.at[to], recvx.at[to], x_send, x_recv.at[i], on_col(1, 0)).start()

    def first_out(who):
        @pl.when((zed == 0) & who)
        def _():
            wc[mine, mine] = win[mine]
            for i in range(len(trunk)):
                set_out(i, wc.at[mine, mine], wr_send, wr_recv)

    first_out(cls == 1)
    send_x(range(begin))

    @pl.when(zed == 0)
    def _():
        send_x(range(begin, near))

    first_out(cls > 1)

    @pl.when((zed == 0) & (cls == LEVEL - 1))
    def _():
        for j in range(2):
            remote(win.at[j], wc.at[2, j], wh_send, wh_recv, (j, col)).start()

    product(half_at, own)

    @pl.when(active & (zed > 0))
    def _():
        wait_for(wc.at[mine, mine], wr_recv)

        @pl.when(branch)
        def _():
            branch_out(wc.at[mine, mine], wr_send, wr_recv)

    @pl.when(zed > 0)
    def _():
        send_x(range(begin, near))

    @pl.when(active)
    def _():
        for c in range(ncol):

            @pl.when((c >= lowest) & (col != c))
            def _():
                wait_for(ybuf.at[c], y_recv.at[c])

            @pl.when(c < lowest)
            def _():
                ybuf[c] = jnp.zeros((rows, LANES), BF16)

        tt[mine, group] = jnp.dot(
            wc[mine, mine], ybuf[...].reshape(size, LANES), preferred_element_type=F32
        ).astype(BF16)
        for d in along_z:
            part = tt.at[mine, group]
            remote(part, part, tz_send, tz_recv, on_z(d)).start()

    beyond = lax.rem(cls + 2, LEVEL)
    twin = cls + 1 - 2 * lax.rem(cls, 2)
    on_beyond = (zed * LEVEL + beyond, col)
    on_twin = (zed * LEVEL + twin, col)

    for i, dy in enumerate(order):
        to = lax.rem(lane_at + dy, near)
        wait_for(recvx.at[to], x_recv.at[i])
        both = own[to] + recvx[to].astype(F32)
        if dy == 0:
            own[to] = both
        else:
            sendy[to] = both.astype(BF16)
            remote(
                sendy.at[to], recvy.at[dy - 1], rs_send, rs_recv, on_col(0, dy)
            ).start()

    def hand_over(some):
        @pl.when(zed > 0)
        def _():
            for piece in some:
                k, side = piece // 2, pl.ds(piece % 2 * (rows // 2), rows // 2)
                remote(
                    win.at[k, side], wl.at[k, cls, side], wl_send, wl_recv.at[0], on_beyond
                ).start()

    hand_over(range(4))

    def pass_on():
        @pl.when(zed == 0)
        def _():
            picks = (
                lax.broadcasted_iota(jnp.int32, (rows, size), 1)
                == lax.broadcasted_iota(jnp.int32, (rows, size), 0) + col * rows
            )
            for k in range(ticks):
                for q in range(LEVEL):
                    wl[k, q] = jnp.where(picks & (k == q), 1.0, 0.0).astype(BF16)

        @pl.when(zed > 0)
        def _():
            wl[:, cls] = win[...]
            there = wl.at[:, beyond]
            wait_for(there, wl_recv.at[0])
            remote(there, there, wl_send, wl_recv.at[2], on_twin).start()

    def settle():
        wait_for(recvy, rs_recv)
        total = own[lane_at]
        for d in range(near - 1):
            total = total + recvy[d].astype(F32)
        pend[...] = rhs[...] - total

    loads[4].wait()

    @pl.when(zed == 0)
    def _():
        settle()
        value = pend[...]
        for q in range(LEVEL):
            part = jnp.concatenate(
                [value[:, q * LANES : (q + 1) * LANES]] * 2, axis=0
            ).T.astype(BF16)
            for t in range(nz):
                pt[q, t] = part[t * width : (t + 1) * width]
        for d in along_z:
            remote(pt.at[:, d], sca, sa_send, sa_recv, on_z(d)).start()
        sca[...] = pt[:, 0]

    def deal(who):
        @pl.when(who & (zed > 0))
        def _():
            wait_for(sca, sa_recv)

        @pl.when(who)
        def _():
            for d in range(1, LEVEL):
                to = lax.rem(cls + d, LEVEL)
                remote(
                    sca.at[to], pin.at[cls], sb_send, sb_recv.at[cls], on_level(d)
                ).start()
            pin[cls] = sca[cls]

    def take(k):
        @pl.when(cls != k)
        def _():
            wait_for(pin.at[k], sb_recv.at[k])

        return pin[k].astype(F32)

    deal(cls == 0)

    @pl.when((zed == 0) & carrier)
    def _():
        @pl.when(cls == 2)
        def _():
            wc[1, 0] = win[0]

        @pl.when(cls < 2)
        def _():
            wait_for(carried, wh_recv)

        for i in range(len(trunk)):
            set_out(i, carried, wo_send, wo_recv)

    lane = lax.broadcasted_iota(jnp.int32, (width, LANES), 1)
    kept = (lane >= parity * rows) & (lane < parity * rows + rows)

    def twice(value):
        return jnp.concatenate([value, value], axis=1)

    def put(n, slot, value):
        turn[n, col, slot] = jnp.where(kept, value, 0.0).astype(BF16)

    def slots(n):
        return pl.ds(0 if n < ticks else 1, 2 if 0 < n < ticks else 1)

    def gather(n):
        part = turn.at[n, col, slots(n)]
        arrived = t_recv.at[n + half_at if n == ticks else n]
        for dx, dy in far:
            remote(part, part, t_send.at[n], arrived, on_col(dx, dy)).start()

    def whole(n, slot):
        return jnp.concatenate(
            [turn[n, 2 * p, slot] + turn[n, 2 * p + 1, slot] for p in range(near)],
            axis=1,
        )

    def window_term(later, k, solved):
        @pl.when(cls != (2 if later == 2 else k))
        def _():
            wait_for(wc.at[later - 1, k], wc_recv.at[later - 1, k])

        return twice(nt_dot(solved, wc[later - 1, k]))

    def fold_term(n, waiting):
        @pl.when(cls != n + 1)
        def _():
            wait_for(tt.at[n], ts_recv.at[n])

        fold = jnp.concatenate([tt[n, g] for g in range(nz)], axis=1)
        return twice(nt_dot(waiting, fold))

    place = pl.multiple_of(zed * width, width)

    def along(k):
        part = sz.at[k, pl.ds(place, width), :]
        for d in along_z:
            remote(part, part, z_send, z_recv.at[k], on_z(d)).start()

    def final(k):
        if k == 0:

            @pl.when(zed > 0)
            def _():
                for way in range(1, 3):
                    wait_for(win, wl_recv.at[way])

        wait_for(sz.at[k, pl.ds(0, (nz - 1) * width)], z_recv.at[k])
        part = nt_dot(wl[k].reshape(LEVEL * rows, size), sz[k])
        for q in range(LEVEL):
            piece = part[q * rows : (q + 1) * rows]
            usum[q] = piece if k == 0 else usum[q] + piece

    def share_fold(who):
        @pl.when(who)
        def _():
            wait_for(tt.at[mine, pl.ds(0, nz - 1)], tz_recv)
            for d in range(1, LEVEL):
                part = tt.at[mine]
                remote(part, part, ts_send, ts_recv.at[mine], on_level(d)).start()

    def share_window(who):
        @pl.when(who)
        def _():
            @pl.when((zed > 0) & jnp.logical_not(branch))
            def _():
                wait_for(carried, wo_recv)

            at = jnp.where(cls == 2, 1, 2), jnp.where(cls == 1, 1, 0)
            for d in range(1, LEVEL):
                remote(carried, carried, wc_send, wc_recv.at[at], on_level(d)).start()

    put(0, 0, take(0))
    gather(0)
    deal(cls > 0)

    @pl.when(branch & carrier)
    def _():
        wait_for(carried, wo_recv)
        branch_out(carried, wo_send, wo_recv)

    share_fold((cls == 1) | (cls == 2))
    share_window(cls == 2)
    def finish():
        for step in range(2):
            part_at = lax.rem(half_at + step, 2)
            wait_for(
                turn.at[ticks, pl.ds(0, near - 1 + step), slots(ticks)],
                t_recv.at[ticks + part_at],
            )
            value = jnp.concatenate(
                [
                    turn[ticks, part_at * near + 2 * p, 1]
                    + turn[ticks, part_at * near + 2 * p + 1, 1]
                    for p in range(near // 2)
                ],
                axis=1,
            )
            lanes = pl.ds(pl.multiple_of(part_at * (size // 2), LANES), size // 2)
            sz[ticks - 1, pl.ds(place, width), lanes] = value
            part = sz.at[ticks - 1, pl.ds(place, width), lanes]
            for d in along_z:
                remote(part, part, z_send, z_recv.at[ticks - 1], on_z(d)).start()

    for n in range(ticks + 1):
        if n == ticks:
            finish()
            for k in range(ticks - 1):
                final(k)
            break
        wait_for(turn.at[n, pl.ds(0, ncol - 1), slots(n)], t_recv.at[n])
        if n == 0:
            for k in range(1, ticks):
                acc[k] = take(k)
        solved = whole(n, 1) if n > 0 else None
        if n < ticks:
            waiting = whole(n, 0)
            put(n + 1, 1, twice(nt_dot(waiting, dinv[n])))
            if n + 1 < ticks:
                value = acc[n + 1] - fold_term(n, waiting)
                if n > 0:
                    value = value - window_term(n + 1, n - 1, solved)
                put(n + 1, 0, value)
            gather(n + 1)
        if n > 0:
            sz[n - 1, pl.ds(place, width), :] = solved
            along(n - 1)
            for later in range(n + 2, ticks):
                acc[later] = acc[later] - window_term(later, n - 1, solved)
        if n == 0:
            share_fold(cls == 3)
            share_window(cls < 2)
        if n == 1:
            hand_over(range(4, 8))

            @pl.when(zed > 0)
            def _():
                remote(win, wl.at[:, cls], wl_send, wl_recv.at[1], on_twin).start()


            @pl.when(zed > 0)
            def _():
                settle()

        if n == 3:
            pass_on()
    final(ticks - 1)

    for d in range(1, LEVEL):
        to = lax.rem(cls + d, LEVEL)
        remote(usum.at[to], ub.at[cls], u_send, u_recv, on_level(d)).start()
    ub[cls] = usum[cls]
    wait_for(ub.at[pl.ds(0, LEVEL - 1)], u_recv)
    for q in range(LEVEL):
        cut = slice(q * LANES, (q + 1) * LANES)
        out_ref[:, cut] = jnp.where(zed == 0, ub[q], pend[:, cut] - ub[q])

    wait_for(recvx, x_send)
    wait_for(recvy, rs_send)
    wait_for(ub.at[pl.ds(0, LEVEL - 1)], u_send)
    wait_for(pin.at[pl.ds(0, LEVEL - 1)], sb_send)

    @pl.when(zed > 0)
    def _():
        for _ in range(3):
            wait_for(win, wl_send)

    for n in range(ticks + 1):
        wait_for(turn.at[n, pl.ds(0, ncol - 1), slots(n)], t_send.at[n])
    for k in range(ticks):
        wait_for(sz.at[k, pl.ds(0, (nz - 1) * width)], z_send)

    @pl.when(zed == 0)
    def _():
        wait_for(pt.at[:, pl.ds(0, nz - 1)], sa_send)

    @pl.when(active & (col >= lowest))
    def _():
        wait_for(ybuf.at[pl.ds(0, ncol - 1)], y_send)

    @pl.when(active)
    def _():
        wait_for(tt.at[mine, pl.ds(0, nz - 1)], tz_send)
        for _ in range(LEVEL - 1):
            wait_for(tt.at[mine], ts_send)

    @pl.when(active & (zed == 0))
    def _():
        for _ in trunk:
            wait_for(wc.at[mine, mine], wr_send)

    @pl.when(carrier & (zed == 0))
    def _():
        for _ in trunk:
            wait_for(carried, wo_send)

    @pl.when(active & branch)
    def _():
        for _ in range(2):
            wait_for(wc.at[mine, mine], wr_send)

    @pl.when(carrier & branch)
    def _():
        for _ in range(2):
            wait_for(carried, wo_send)

    @pl.when((zed == 0) & (cls == LEVEL - 1))
    def _():
        wait_for(wc.at[2, pl.ds(0, 2)], wh_send)

    @pl.when(carrier)
    def _():
        wait_for(wc.at[0], wc_send)


def per_device(right_side, prior_panel, prior_solved, window_panel, diag_inverse):
    rows, columns = right_side.shape[2:]
    size = prior_panel.shape[4]
    ticks = window_panel.shape[2]
    ncol = lax.axis_size("col")
    nz = lax.axis_size("row") // LEVEL
    width = LANES // nz
    near = ncol // 2
    dma = pltpu.SemaphoreType.DMA
    vmem = pltpu.VMEM
    out = pl.pallas_call(
        functools.partial(kernel, nz, ncol),
        out_shape=jax.ShapeDtypeStruct((rows, columns), F32),
        in_specs=[pl.BlockSpec(memory_space=pl.ANY)] * 5,
        out_specs=pl.BlockSpec(memory_space=pltpu.VMEM),
        scratch_shapes=[
            vmem((rows, columns), F32),
            vmem((size, size), BF16),
            vmem((size, columns), BF16),
            vmem((ticks, rows, size), BF16),
            vmem((ticks, rows, size), BF16),
            vmem((near, rows, columns), BF16),
            vmem((near, rows, columns), BF16),
            vmem((near, rows, columns), F32),
            vmem((near, rows, columns), BF16),
            vmem((near - 1, rows, columns), BF16),
            vmem((rows, columns), F32),
            vmem((LEVEL, nz, width, LANES), BF16),
            vmem((LEVEL, width, LANES), BF16),
            vmem((LEVEL, width, LANES), BF16),
            vmem((ticks, width, LANES), F32),
            vmem((ticks + 1, ncol, 2, width, LANES), BF16),
            vmem((ticks, LANES, size), BF16),
            vmem((ticks, LEVEL, rows, size), BF16),
            vmem((LEVEL - 1, LEVEL - 1, rows, size), BF16),
            vmem((ncol, rows, LANES), BF16),
            vmem((LEVEL - 1, nz, rows, LANES), BF16),
            vmem((LEVEL, rows, LANES), F32),
            vmem((LEVEL, rows, LANES), F32),
            dma((5,)),
            dma,
            dma((near,)),
            dma,
            dma,
            dma,
            dma,
            dma,
            dma((LEVEL,)),
            dma,
            dma,
            dma,
            dma,
            dma,
            dma,
            dma,
            dma((LEVEL - 1, LEVEL - 1)),
            dma,
            dma((3,)),
            dma,
            dma((ncol,)),
            dma,
            dma,
            dma,
            dma((LEVEL - 1,)),
            dma((ticks + 1,)),
            dma((ticks + 2,)),
            dma,
            dma((ticks,)),
            dma,
            dma,
        ],
        compiler_params=pltpu.CompilerParams(
            collective_id=0,
            has_side_effects=True,
            vmem_limit_bytes=60 * 1024 * 1024,
        ),
    )(
        right_side.reshape(rows, columns),
        prior_panel.reshape(size, size),
        prior_solved.reshape(size, columns),
        window_panel.reshape(ticks, rows, size),
        diag_inverse,
    )
    return out.reshape(right_side.shape)


def solution(mesh):
    return jax.shard_map(
        per_device,
        mesh=mesh,
        in_specs=(
            P(None, "row", "col", None),
            P(None, "row", None, "col", None, None),
            P(None, "col", None, None),
            P(None, "row", None, "col", None),
            P(None, "col", None),
        ),
        out_specs=P(None, "row", "col", None),
        check_vma=False,
    )
```

```python
import functools

import jax
import jax.numpy as jnp
from jax import lax
from jax.experimental import pallas as pl
from jax.experimental.pallas import tpu as pltpu
from jax.sharding import PartitionSpec as P

MESH = pl.DeviceIdType.MESH
F32 = jnp.float32
BF16 = jnp.bfloat16
LEVEL = 4
LANES = 128


def nt_dot(a, b):
    return lax.dot_general(
        a, b, (((1,), (1,)), ((), ())), preferred_element_type=F32
    )


def kernel(
    nz,
    ncol,
    rhs_h,
    panel_h,
    prior_h,
    win_h,
    dinv_h,
    out_ref,
    rhs,
    panel,
    prior,
    win,
    dinv,
    sendx,
    sendy,
    own,
    recvx,
    recvy,
    pend,
    pt,
    sca,
    pin,
    acc,
    turn,
    sz,
    wl,
    wc,
    ybuf,
    tt,
    usum,
    ub,
    load_sem,
    x_send,
    x_recv,
    rs_send,
    rs_recv,
    sa_send,
    sa_recv,
    sb_send,
    sb_recv,
    wr_send,
    wr_recv,
    wh_send,
    wh_recv,
    wo_send,
    wo_recv,
    wc_send,
    wc_recv,
    wl_send,
    wl_recv,
    y_send,
    y_recv,
    tz_send,
    tz_recv,
    ts_send,
    ts_recv,
    t_send,
    t_recv,
    z_send,
    z_recv,
    u_send,
    u_recv,
):
    row = lax.axis_index("row")
    col = lax.axis_index("col")
    zed = row // LEVEL
    cls = row % LEVEL
    ticks, rows, size = win.shape
    width = pin.shape[1]
    columns = rhs.shape[1]
    near = ncol // 2
    half_at = col // near
    lane_at = col % near
    parity = col % 2

    loads = [
        pltpu.make_async_copy(src, dst, load_sem.at[i])
        for i, (src, dst) in enumerate(
            ((prior_h, prior), (panel_h, panel), (dinv_h, dinv), (win_h, win), (rhs_h, rhs))
        )
    ]
    for load in loads:
        load.start()

    far = sorted(
        ((dx, dy) for dx in range(2) for dy in range(near) if dx or dy),
        key=lambda p: -(2 * p[0] + min(p[1], near - p[1])),
    )

    def on_col(dx, dy):
        return (row, lax.rem(half_at + dx, 2) * near + lax.rem(lane_at + dy, near))

    def on_z(d):
        return (lax.rem(zed + d, nz) * LEVEL + cls, col)

    along_z = sorted(range(1, nz), key=lambda d: -min(d, nz - d))

    def on_level(d):
        return (zed * LEVEL + lax.rem(cls + d, LEVEL), col)

    def remote(src, dst, send, recv, device):
        return pltpu.make_async_remote_copy(
            src_ref=src,
            dst_ref=dst,
            send_sem=send,
            recv_sem=recv,
            device_id=device,
            device_id_type=MESH,
        )

    def wait_for(ref, sem):
        pltpu.make_async_copy(ref, ref, sem).wait()

    barrier = pltpu.get_barrier_semaphore()
    friends = [(2 * dx + min(dy, near - dy), on_col(dx, dy)) for dx, dy in far]
    friends += [(min(d, nz - d), on_z(d)) for d in along_z]
    friends += [(1, on_level(d)) for d in range(1, LEVEL)]
    for _, friend in sorted(friends, key=lambda p: -p[0]):
        pl.semaphore_signal(barrier, inc=1, device_id=friend, device_id_type=MESH)

    loads[0].wait()
    loads[1].wait()
    per_block = min(4, near)

    def product(at, out):
        def body(i, carry):
            start = pl.multiple_of((at * near + i * per_block) * rows, per_block * rows)
            part = jnp.dot(
                panel[pl.ds(start, per_block * rows), :],
                prior[...],
                preferred_element_type=F32,
            ).astype(out.dtype)
            for t in range(per_block):
                out[i * per_block + t] = part[t * rows : (t + 1) * rows]
            return carry

        lax.fori_loop(0, near // per_block, body, 0)

    order = sorted(range(near), key=lambda d: -min(d, near - d))
    product(1 - half_at, sendx)
    loads[2].wait()
    loads[3].wait()
    active = cls >= 1
    mine = jnp.maximum(cls - 1, 0)
    carrier = cls < LEVEL - 1
    carried = wc.at[jnp.where(cls == 2, 1, 2), jnp.where(cls == 1, 1, 0)]
    begin = near // 2
    trunk = sorted(range(2, nz, 2), key=lambda d: -min(d, nz - d)) or [1]
    branch = (zed % 4 == 2) if nz > 2 else (zed < 0)

    def set_out(i, block, send, recv):
        if i in range(len(trunk)):
            remote(block, block, send, recv, on_z(trunk[i])).start()

    def branch_out(block, send, recv):
        for d in (1, nz - 1):
            remote(block, block, send, recv, on_z(d)).start()

    group = nz - 1 - zed
    lowest = group * (size // nz) // rows
    tile = pl.ds(pl.multiple_of(group * LANES, LANES), LANES)
    pl.semaphore_wait(barrier, len(friends))

    @pl.when(active & (col >= lowest))
    def _():
        ybuf[col] = dinv[mine, :, tile]
        for dx, dy in far:
            remote(
                ybuf.at[col], ybuf.at[col], y_send, y_recv.at[col], on_col(dx, dy)
            ).start()

    def send_x(some):
        for i in some:
            to = lax.rem(lane_at + order[i], near)
            remote(sendx.at[to], recvx.at[to], x_send, x_recv.at[i], on_col(1, 0)).start()

    def first_out(who):
        @pl.when((zed == 0) & who)
        def _():
            wc[mine, mine] = win[mine]
            for i in range(len(trunk)):
                set_out(i, wc.at[mine, mine], wr_send, wr_recv)

    first_out(cls == 1)
    send_x(range(begin))

    @pl.when(zed == 0)
    def _():
        send_x(range(begin, near))

    first_out(cls > 1)

    @pl.when((zed == 0) & (cls == LEVEL - 1))
    def _():
        for j in range(2):
            remote(win.at[j], wc.at[2, j], wh_send, wh_recv, (j, col)).start()

    product(half_at, own)

    @pl.when(active & (zed > 0))
    def _():
        wait_for(wc.at[mine, mine], wr_recv)

        @pl.when(branch)
        def _():
            branch_out(wc.at[mine, mine], wr_send, wr_recv)

    @pl.when(zed > 0)
    def _():
        send_x(range(begin, near))

    def fold_here(who):
        @pl.when(active & who)
        def _():
            for c in range(ncol):

                @pl.when((c >= lowest) & (col != c))
                def _():
                    wait_for(ybuf.at[c], y_recv.at[c])

                @pl.when(c < lowest)
                def _():
                    ybuf[c] = jnp.zeros((rows, LANES), BF16)

            tt[mine, group] = jnp.dot(
                wc[mine, mine], ybuf[...].reshape(size, LANES), preferred_element_type=F32
            ).astype(BF16)
            for d in along_z:
                part = tt.at[mine, group]
                remote(part, part, tz_send, tz_recv, on_z(d)).start()

    fold_here(zed > 0)

    beyond = lax.rem(cls + 2, LEVEL)
    twin = cls + 1 - 2 * lax.rem(cls, 2)
    on_beyond = (zed * LEVEL + beyond, col)
    on_twin = (zed * LEVEL + twin, col)

    for i, dy in enumerate(order):
        to = lax.rem(lane_at + dy, near)
        wait_for(recvx.at[to], x_recv.at[i])
        both = own[to] + recvx[to].astype(F32)
        if dy == 0:
            own[to] = both
        else:
            sendy[to] = both.astype(BF16)
            remote(
                sendy.at[to], recvy.at[dy - 1], rs_send, rs_recv, on_col(0, dy)
            ).start()

    def hand_over(some):
        @pl.when(zed > 0)
        def _():
            for piece in some:
                k, side = piece // 2, pl.ds(piece % 2 * (rows // 2), rows // 2)
                remote(
                    win.at[k, side], wl.at[k, cls, side], wl_send, wl_recv.at[0], on_beyond
                ).start()

    hand_over(range(4))

    def pass_on():
        @pl.when(zed == 0)
        def _():
            picks = (
                lax.broadcasted_iota(jnp.int32, (rows, size), 1)
                == lax.broadcasted_iota(jnp.int32, (rows, size), 0) + col * rows
            )
            for k in range(ticks):
                for q in range(LEVEL):
                    wl[k, q] = jnp.where(picks & (k == q), 1.0, 0.0).astype(BF16)

        @pl.when(zed > 0)
        def _():
            wl[:, cls] = win[...]
            there = wl.at[:, beyond]
            wait_for(there, wl_recv.at[0])
            remote(there, there, wl_send, wl_recv.at[2], on_twin).start()

    def settle():
        wait_for(recvy, rs_recv)
        total = own[lane_at]
        for d in range(near - 1):
            total = total + recvy[d].astype(F32)
        pend[...] = rhs[...] - total

    loads[4].wait()

    @pl.when(zed == 0)
    def _():
        settle()
        value = pend[...]
        for q in range(LEVEL):
            part = jnp.concatenate(
                [value[:, q * LANES : (q + 1) * LANES]] * 2, axis=0
            ).T.astype(BF16)
            for t in range(nz):
                pt[q, t] = part[t * width : (t + 1) * width]
        for d in along_z:
            remote(pt.at[:, d], sca, sa_send, sa_recv, on_z(d)).start()
        sca[...] = pt[:, 0]

    def deal(who):
        @pl.when(who & (zed > 0))
        def _():
            wait_for(sca, sa_recv)

        @pl.when(who)
        def _():
            for d in range(1, LEVEL):
                to = lax.rem(cls + d, LEVEL)
                remote(
                    sca.at[to], pin.at[cls], sb_send, sb_recv.at[cls], on_level(d)
                ).start()
            pin[cls] = sca[cls]

    def take(k):
        @pl.when(cls != k)
        def _():
            wait_for(pin.at[k], sb_recv.at[k])

        return pin[k].astype(F32)

    deal(cls == 0)
    fold_here(zed == 0)

    @pl.when((zed == 0) & carrier)
    def _():
        @pl.when(cls == 2)
        def _():
            wc[1, 0] = win[0]

        @pl.when(cls < 2)
        def _():
            wait_for(carried, wh_recv)

        for i in range(len(trunk)):
            set_out(i, carried, wo_send, wo_recv)

    lane = lax.broadcasted_iota(jnp.int32, (width, LANES), 1)
    kept = (lane >= parity * rows) & (lane < parity * rows + rows)

    def twice(value):
        return jnp.concatenate([value, value], axis=1)

    def put(n, slot, value):
        turn[n, col, slot] = jnp.where(kept, value, 0.0).astype(BF16)

    def slots(n):
        return pl.ds(0 if n < ticks else 1, 2 if 0 < n < ticks else 1)

    def gather(n):
        part = turn.at[n, col, slots(n)]
        arrived = t_recv.at[n + half_at if n == ticks else n]
        for dx, dy in far:
            remote(part, part, t_send.at[n], arrived, on_col(dx, dy)).start()

    def whole(n, slot):
        return jnp.concatenate(
            [turn[n, 2 * p, slot] + turn[n, 2 * p + 1, slot] for p in range(near)],
            axis=1,
        )

    def window_term(later, k, solved):
        @pl.when(cls != (2 if later == 2 else k))
        def _():
            wait_for(wc.at[later - 1, k], wc_recv.at[later - 1, k])

        return twice(nt_dot(solved, wc[later - 1, k]))

    def fold_term(n, waiting):
        @pl.when(cls != n + 1)
        def _():
            wait_for(tt.at[n], ts_recv.at[n])

        fold = jnp.concatenate([tt[n, g] for g in range(nz)], axis=1)
        return twice(nt_dot(waiting, fold))

    place = pl.multiple_of(zed * width, width)

    def along(k):
        part = sz.at[k, pl.ds(place, width), :]
        for d in along_z:
            remote(part, part, z_send, z_recv.at[k], on_z(d)).start()

    def final(k):
        if k == 0:

            @pl.when(zed > 0)
            def _():
                for way in range(1, 3):
                    wait_for(win, wl_recv.at[way])

        wait_for(sz.at[k, pl.ds(0, (nz - 1) * width)], z_recv.at[k])
        part = nt_dot(wl[k].reshape(LEVEL * rows, size), sz[k])
        for q in range(LEVEL):
            piece = part[q * rows : (q + 1) * rows]
            usum[q] = piece if k == 0 else usum[q] + piece

    def share_fold(who):
        @pl.when(who)
        def _():
            wait_for(tt.at[mine, pl.ds(0, nz - 1)], tz_recv)
            for d in range(1, LEVEL):
                part = tt.at[mine]
                remote(part, part, ts_send, ts_recv.at[mine], on_level(d)).start()

    def share_window(who):
        @pl.when(who)
        def _():
            @pl.when((zed > 0) & jnp.logical_not(branch))
            def _():
                wait_for(carried, wo_recv)

            at = jnp.where(cls == 2, 1, 2), jnp.where(cls == 1, 1, 0)
            for d in range(1, LEVEL):
                remote(carried, carried, wc_send, wc_recv.at[at], on_level(d)).start()

    put(0, 0, take(0))
    gather(0)
    deal(cls > 0)

    @pl.when(branch & carrier)
    def _():
        wait_for(carried, wo_recv)
        branch_out(carried, wo_send, wo_recv)

    share_fold((cls == 1) | (cls == 2))
    share_window(cls == 2)
    def finish():
        for step in range(2):
            part_at = lax.rem(half_at + step, 2)
            wait_for(
                turn.at[ticks, pl.ds(0, near - 1 + step), slots(ticks)],
                t_recv.at[ticks + part_at],
            )
            value = jnp.concatenate(
                [
                    turn[ticks, part_at * near + 2 * p, 1]
                    + turn[ticks, part_at * near + 2 * p + 1, 1]
                    for p in range(near // 2)
                ],
                axis=1,
            )
            lanes = pl.ds(pl.multiple_of(part_at * (size // 2), LANES), size // 2)
            sz[ticks - 1, pl.ds(place, width), lanes] = value
            part = sz.at[ticks - 1, pl.ds(place, width), lanes]
            for d in along_z:
                remote(part, part, z_send, z_recv.at[ticks - 1], on_z(d)).start()

    for n in range(ticks + 1):
        if n == ticks:
            finish()
            for k in range(ticks - 1):
                final(k)
            break
        wait_for(turn.at[n, pl.ds(0, ncol - 1), slots(n)], t_recv.at[n])
        if n == 0:
            for k in range(1, ticks):
                acc[k] = take(k)
        solved = whole(n, 1) if n > 0 else None
        if n < ticks:
            waiting = whole(n, 0)
            put(n + 1, 1, twice(nt_dot(waiting, dinv[n])))
            if n + 1 < ticks:
                value = acc[n + 1] - fold_term(n, waiting)
                if n > 0:
                    value = value - window_term(n + 1, n - 1, solved)
                put(n + 1, 0, value)
            gather(n + 1)
        if n > 0:
            sz[n - 1, pl.ds(place, width), :] = solved
            along(n - 1)
            for later in range(n + 2, ticks):
                acc[later] = acc[later] - window_term(later, n - 1, solved)
        if n == 0:
            share_fold(cls == 3)
            share_window(cls < 2)
        if n == 1:
            hand_over(range(4, 8))

            @pl.when(zed > 0)
            def _():
                remote(win, wl.at[:, cls], wl_send, wl_recv.at[1], on_twin).start()


            @pl.when(zed > 0)
            def _():
                settle()

        if n == 3:
            pass_on()
    final(ticks - 1)

    for d in range(1, LEVEL):
        to = lax.rem(cls + d, LEVEL)
        remote(usum.at[to], ub.at[cls], u_send, u_recv, on_level(d)).start()
    ub[cls] = usum[cls]
    wait_for(ub.at[pl.ds(0, LEVEL - 1)], u_recv)
    for q in range(LEVEL):
        cut = slice(q * LANES, (q + 1) * LANES)
        out_ref[:, cut] = jnp.where(zed == 0, ub[q], pend[:, cut] - ub[q])

    wait_for(recvx, x_send)
    wait_for(recvy, rs_send)
    wait_for(ub.at[pl.ds(0, LEVEL - 1)], u_send)
    wait_for(pin.at[pl.ds(0, LEVEL - 1)], sb_send)

    @pl.when(zed > 0)
    def _():
        for _ in range(3):
            wait_for(win, wl_send)

    for n in range(ticks + 1):
        wait_for(turn.at[n, pl.ds(0, ncol - 1), slots(n)], t_send.at[n])
    for k in range(ticks):
        wait_for(sz.at[k, pl.ds(0, (nz - 1) * width)], z_send)

    @pl.when(zed == 0)
    def _():
        wait_for(pt.at[:, pl.ds(0, nz - 1)], sa_send)

    @pl.when(active & (col >= lowest))
    def _():
        wait_for(ybuf.at[pl.ds(0, ncol - 1)], y_send)

    @pl.when(active)
    def _():
        wait_for(tt.at[mine, pl.ds(0, nz - 1)], tz_send)
        for _ in range(LEVEL - 1):
            wait_for(tt.at[mine], ts_send)

    @pl.when(active & (zed == 0))
    def _():
        for _ in trunk:
            wait_for(wc.at[mine, mine], wr_send)

    @pl.when(carrier & (zed == 0))
    def _():
        for _ in trunk:
            wait_for(carried, wo_send)

    @pl.when(active & branch)
    def _():
        for _ in range(2):
            wait_for(wc.at[mine, mine], wr_send)

    @pl.when(carrier & branch)
    def _():
        for _ in range(2):
            wait_for(carried, wo_send)

    @pl.when((zed == 0) & (cls == LEVEL - 1))
    def _():
        wait_for(wc.at[2, pl.ds(0, 2)], wh_send)

    @pl.when(carrier)
    def _():
        wait_for(wc.at[0], wc_send)


def per_device(right_side, prior_panel, prior_solved, window_panel, diag_inverse):
    rows, columns = right_side.shape[2:]
    size = prior_panel.shape[4]
    ticks = window_panel.shape[2]
    ncol = lax.axis_size("col")
    nz = lax.axis_size("row") // LEVEL
    width = LANES // nz
    near = ncol // 2
    dma = pltpu.SemaphoreType.DMA
    vmem = pltpu.VMEM
    out = pl.pallas_call(
        functools.partial(kernel, nz, ncol),
        out_shape=jax.ShapeDtypeStruct((rows, columns), F32),
        in_specs=[pl.BlockSpec(memory_space=pl.ANY)] * 5,
        out_specs=pl.BlockSpec(memory_space=pltpu.VMEM),
        scratch_shapes=[
            vmem((rows, columns), F32),
            vmem((size, size), BF16),
            vmem((size, columns), BF16),
            vmem((ticks, rows, size), BF16),
            vmem((ticks, rows, size), BF16),
            vmem((near, rows, columns), BF16),
            vmem((near, rows, columns), BF16),
            vmem((near, rows, columns), F32),
            vmem((near, rows, columns), BF16),
            vmem((near - 1, rows, columns), BF16),
            vmem((rows, columns), F32),
            vmem((LEVEL, nz, width, LANES), BF16),
            vmem((LEVEL, width, LANES), BF16),
            vmem((LEVEL, width, LANES), BF16),
            vmem((ticks, width, LANES), F32),
            vmem((ticks + 1, ncol, 2, width, LANES), BF16),
            vmem((ticks, LANES, size), BF16),
            vmem((ticks, LEVEL, rows, size), BF16),
            vmem((LEVEL - 1, LEVEL - 1, rows, size), BF16),
            vmem((ncol, rows, LANES), BF16),
            vmem((LEVEL - 1, nz, rows, LANES), BF16),
            vmem((LEVEL, rows, LANES), F32),
            vmem((LEVEL, rows, LANES), F32),
            dma((5,)),
            dma,
            dma((near,)),
            dma,
            dma,
            dma,
            dma,
            dma,
            dma((LEVEL,)),
            dma,
            dma,
            dma,
            dma,
            dma,
            dma,
            dma,
            dma((LEVEL - 1, LEVEL - 1)),
            dma,
            dma((3,)),
            dma,
            dma((ncol,)),
            dma,
            dma,
            dma,
            dma((LEVEL - 1,)),
            dma((ticks + 1,)),
            dma((ticks + 2,)),
            dma,
            dma((ticks,)),
            dma,
            dma,
        ],
        compiler_params=pltpu.CompilerParams(
            collective_id=0,
            has_side_effects=True,
            vmem_limit_bytes=60 * 1024 * 1024,
        ),
    )(
        right_side.reshape(rows, columns),
        prior_panel.reshape(size, size),
        prior_solved.reshape(size, columns),
        window_panel.reshape(ticks, rows, size),
        diag_inverse,
    )
    return out.reshape(right_side.shape)


def solution(mesh):
    return jax.shard_map(
        per_device,
        mesh=mesh,
        in_specs=(
            P(None, "row", "col", None),
            P(None, "row", None, "col", None, None),
            P(None, "col", None, None),
            P(None, "row", None, "col", None),
            P(None, "col", None),
        ),
        out_specs=P(None, "row", "col", None),
        check_vma=False,
    )
```

```python
import functools

import jax
import jax.numpy as jnp
from jax import lax
from jax.experimental import pallas as pl
from jax.experimental.pallas import tpu as pltpu
from jax.sharding import PartitionSpec as P

MESH = pl.DeviceIdType.MESH
F32 = jnp.float32
BF16 = jnp.bfloat16
LEVEL = 4
LANES = 128


def nt_dot(a, b):
    return lax.dot_general(
        a, b, (((1,), (1,)), ((), ())), preferred_element_type=F32
    )


def kernel(
    nz,
    ncol,
    rhs_h,
    panel_h,
    prior_h,
    win_h,
    dinv_h,
    out_ref,
    rhs,
    panel,
    prior,
    win,
    dinv,
    sendx,
    sendy,
    own,
    recvx,
    recvy,
    pend,
    pt,
    sca,
    pin,
    acc,
    turn,
    sz,
    wl,
    wc,
    ybuf,
    tt,
    usum,
    ub,
    load_sem,
    x_send,
    x_recv,
    rs_send,
    rs_recv,
    sa_send,
    sa_recv,
    sb_send,
    sb_recv,
    wr_send,
    wr_recv,
    wh_send,
    wh_recv,
    wo_send,
    wo_recv,
    wc_send,
    wc_recv,
    wl_send,
    wl_recv,
    y_send,
    y_recv,
    tz_send,
    tz_recv,
    ts_send,
    ts_recv,
    t_send,
    t_recv,
    z_send,
    z_recv,
    u_send,
    u_recv,
):
    row = lax.axis_index("row")
    col = lax.axis_index("col")
    zed = row // LEVEL
    cls = row % LEVEL
    ticks, rows, size = win.shape
    width = pin.shape[1]
    columns = rhs.shape[1]
    near = ncol // 2
    half_at = col // near
    lane_at = col % near
    parity = col % 2

    loads = [
        pltpu.make_async_copy(src, dst, load_sem.at[i])
        for i, (src, dst) in enumerate(
            ((prior_h, prior), (panel_h, panel), (dinv_h, dinv), (win_h, win), (rhs_h, rhs))
        )
    ]
    for load in loads:
        load.start()

    far = sorted(
        ((dx, dy) for dx in range(2) for dy in range(near) if dx or dy),
        key=lambda p: -(2 * p[0] + min(p[1], near - p[1])),
    )

    def on_col(dx, dy):
        return (row, lax.rem(half_at + dx, 2) * near + lax.rem(lane_at + dy, near))

    def on_z(d):
        return (lax.rem(zed + d, nz) * LEVEL + cls, col)

    along_z = sorted(range(1, nz), key=lambda d: -min(d, nz - d))

    def on_level(d):
        return (zed * LEVEL + lax.rem(cls + d, LEVEL), col)

    def remote(src, dst, send, recv, device):
        return pltpu.make_async_remote_copy(
            src_ref=src,
            dst_ref=dst,
            send_sem=send,
            recv_sem=recv,
            device_id=device,
            device_id_type=MESH,
        )

    def wait_for(ref, sem):
        pltpu.make_async_copy(ref, ref, sem).wait()

    barrier = pltpu.get_barrier_semaphore()
    friends = [(2 * dx + min(dy, near - dy), on_col(dx, dy)) for dx, dy in far]
    friends += [(min(d, nz - d), on_z(d)) for d in along_z]
    friends += [(1, on_level(d)) for d in range(1, LEVEL)]
    for _, friend in sorted(friends, key=lambda p: -p[0]):
        pl.semaphore_signal(barrier, inc=1, device_id=friend, device_id_type=MESH)

    loads[0].wait()
    loads[1].wait()
    per_block = min(4, near)

    def product(at, out):
        def body(i, carry):
            start = pl.multiple_of((at * near + i * per_block) * rows, per_block * rows)
            part = jnp.dot(
                panel[pl.ds(start, per_block * rows), :],
                prior[...],
                preferred_element_type=F32,
            ).astype(out.dtype)
            for t in range(per_block):
                out[i * per_block + t] = part[t * rows : (t + 1) * rows]
            return carry

        lax.fori_loop(0, near // per_block, body, 0)

    order = sorted(range(near), key=lambda d: -min(d, near - d))
    product(1 - half_at, sendx)
    loads[2].wait()
    loads[3].wait()
    active = cls >= 1
    mine = jnp.maximum(cls - 1, 0)
    carrier = cls < LEVEL - 1
    carried = wc.at[jnp.where(cls == 2, 1, 2), jnp.where(cls == 1, 1, 0)]
    begin = near // 2
    trunk = sorted(range(2, nz, 2), key=lambda d: -min(d, nz - d)) or [1]
    branch = (zed % 4 == 2) if nz > 2 else (zed < 0)

    def set_out(i, block, send, recv):
        if i in range(len(trunk)):
            remote(block, block, send, recv, on_z(trunk[i])).start()

    def branch_out(block, send, recv):
        for d in (1, nz - 1):
            remote(block, block, send, recv, on_z(d)).start()

    group = nz - 1 - zed
    lowest = group * (size // nz) // rows
    tile = pl.ds(pl.multiple_of(group * LANES, LANES), LANES)
    pl.semaphore_wait(barrier, len(friends))

    @pl.when(active & (col >= lowest))
    def _():
        ybuf[col] = dinv[mine, :, tile]
        for dx, dy in far:
            remote(
                ybuf.at[col], ybuf.at[col], y_send, y_recv.at[col], on_col(dx, dy)
            ).start()

    def send_x(some):
        for i in some:
            to = lax.rem(lane_at + order[i], near)
            remote(sendx.at[to], recvx.at[to], x_send, x_recv.at[i], on_col(1, 0)).start()

    def first_out(who):
        @pl.when((zed == 0) & who)
        def _():
            wc[mine, mine] = win[mine]
            for i in range(len(trunk)):
                set_out(i, wc.at[mine, mine], wr_send, wr_recv)

    first_out(cls == 1)
    send_x(range(begin))

    @pl.when(zed == 0)
    def _():
        send_x(range(begin, near))

    first_out(cls > 1)

    @pl.when((zed == 0) & (cls == LEVEL - 1))
    def _():
        for j in range(2):
            remote(win.at[j], wc.at[2, j], wh_send, wh_recv, (j, col)).start()

    product(half_at, own)

    @pl.when(active & (zed > 0))
    def _():
        wait_for(wc.at[mine, mine], wr_recv)

        @pl.when(branch)
        def _():
            branch_out(wc.at[mine, mine], wr_send, wr_recv)

    @pl.when(zed > 0)
    def _():
        send_x(range(begin, near))

    def fold_here(who):
        @pl.when(active & who)
        def _():
            for c in range(ncol):

                @pl.when((c >= lowest) & (col != c))
                def _():
                    wait_for(ybuf.at[c], y_recv.at[c])

                @pl.when(c < lowest)
                def _():
                    ybuf[c] = jnp.zeros((rows, LANES), BF16)

            tt[mine, group] = jnp.dot(
                wc[mine, mine], ybuf[...].reshape(size, LANES), preferred_element_type=F32
            ).astype(BF16)
            for d in along_z:
                part = tt.at[mine, group]
                remote(part, part, tz_send, tz_recv, on_z(d)).start()

    fold_here(zed > 0)

    beyond = lax.rem(cls + 2, LEVEL)
    twin = cls + 1 - 2 * lax.rem(cls, 2)
    on_beyond = (zed * LEVEL + beyond, col)
    on_twin = (zed * LEVEL + twin, col)

    for i, dy in enumerate(order):
        to = lax.rem(lane_at + dy, near)
        wait_for(recvx.at[to], x_recv.at[i])
        both = own[to] + recvx[to].astype(F32)
        if dy == 0:
            own[to] = both
        else:
            sendy[to] = both.astype(BF16)
            remote(
                sendy.at[to], recvy.at[dy - 1], rs_send, rs_recv, on_col(0, dy)
            ).start()

    def hand_over(some):
        @pl.when(zed > 0)
        def _():
            for piece in some:
                k, side = piece // 2, pl.ds(piece % 2 * (rows // 2), rows // 2)
                remote(
                    win.at[k, side], wl.at[k, cls, side], wl_send, wl_recv.at[0], on_beyond
                ).start()

    hand_over(range(4))

    def pass_on():
        @pl.when(zed == 0)
        def _():
            picks = (
                lax.broadcasted_iota(jnp.int32, (rows, size), 1)
                == lax.broadcasted_iota(jnp.int32, (rows, size), 0) + col * rows
            )
            for k in range(ticks):
                for q in range(LEVEL):
                    wl[k, q] = jnp.where(picks & (k == q), 1.0, 0.0).astype(BF16)

        @pl.when(zed > 0)
        def _():
            wl[:, cls] = win[...]
            there = wl.at[:, beyond]
            wait_for(there, wl_recv.at[0])
            remote(there, there, wl_send, wl_recv.at[2], on_twin).start()

    def settle():
        wait_for(recvy, rs_recv)
        total = own[lane_at]
        for d in range(near - 1):
            total = total + recvy[d].astype(F32)
        pend[...] = rhs[...] - total

    loads[4].wait()

    @pl.when(zed == 0)
    def _():
        settle()
        value = pend[...]
        for q in range(LEVEL):
            part = jnp.concatenate(
                [value[:, q * LANES : (q + 1) * LANES]] * 2, axis=0
            ).T.astype(BF16)
            for t in range(nz):
                pt[q, t] = part[t * width : (t + 1) * width]
        for d in along_z:
            remote(pt.at[:, d], sca, sa_send, sa_recv, on_z(d)).start()
        sca[...] = pt[:, 0]

    def deal(who):
        @pl.when(who & (zed > 0))
        def _():
            wait_for(sca, sa_recv)

        @pl.when(who)
        def _():
            for d in range(1, LEVEL):
                to = lax.rem(cls + d, LEVEL)
                remote(
                    sca.at[to], pin.at[cls], sb_send, sb_recv.at[cls], on_level(d)
                ).start()
            pin[cls] = sca[cls]

    def take(k):
        @pl.when(cls != k)
        def _():
            wait_for(pin.at[k], sb_recv.at[k])

        return pin[k].astype(F32)

    deal(cls == 0)
    fold_here(zed == 0)

    @pl.when((zed == 0) & carrier)
    def _():
        @pl.when(cls == 2)
        def _():
            wc[1, 0] = win[0]

        @pl.when(cls < 2)
        def _():
            wait_for(carried, wh_recv)

        for i in range(len(trunk)):
            set_out(i, carried, wo_send, wo_recv)

    lane = lax.broadcasted_iota(jnp.int32, (width, LANES), 1)
    kept = (lane >= parity * rows) & (lane < parity * rows + rows)

    def twice(value):
        return jnp.concatenate([value, value], axis=1)

    def put(n, slot, value):
        turn[n, col, slot] = jnp.where(kept, value, 0.0).astype(BF16)

    def slots(n):
        return pl.ds(0 if n < ticks else 1, 2 if 0 < n < ticks else 1)

    def gather(n):
        part = turn.at[n, col, slots(n)]
        arrived = t_recv.at[n + half_at if n == ticks else n]
        for dx, dy in far:
            remote(part, part, t_send.at[n], arrived, on_col(dx, dy)).start()

    def whole(n, slot):
        return jnp.concatenate(
            [turn[n, 2 * p, slot] + turn[n, 2 * p + 1, slot] for p in range(near)],
            axis=1,
        )

    def window_term(later, k, solved):
        @pl.when(cls != (2 if later == 2 else k))
        def _():
            wait_for(wc.at[later - 1, k], wc_recv.at[later - 1, k])

        return twice(nt_dot(solved, wc[later - 1, k]))

    def fold_term(n, waiting):
        @pl.when(cls != n + 1)
        def _():
            wait_for(tt.at[n], ts_recv.at[n])

        fold = jnp.concatenate([tt[n, g] for g in range(nz)], axis=1)
        return twice(nt_dot(waiting, fold))

    place = pl.multiple_of(zed * width, width)

    def along(k):
        part = sz.at[k, pl.ds(place, width), :]
        for d in along_z:
            remote(part, part, z_send, z_recv.at[k], on_z(d)).start()

    def final(k):
        if k == 0:

            @pl.when(zed > 0)
            def _():
                for way in range(1, 3):
                    wait_for(win, wl_recv.at[way])

        wait_for(sz.at[k, pl.ds(0, (nz - 1) * width)], z_recv.at[k])
        part = nt_dot(wl[k].reshape(LEVEL * rows, size), sz[k])
        for q in range(LEVEL):
            piece = part[q * rows : (q + 1) * rows]
            usum[q] = piece if k == 0 else usum[q] + piece

    def share_fold(who):
        @pl.when(who)
        def _():
            wait_for(tt.at[mine, pl.ds(0, nz - 1)], tz_recv)
            for d in range(1, LEVEL):
                part = tt.at[mine]
                remote(part, part, ts_send, ts_recv.at[mine], on_level(d)).start()

    def share_window(who):
        @pl.when(who)
        def _():
            @pl.when((zed > 0) & jnp.logical_not(branch))
            def _():
                wait_for(carried, wo_recv)

            at = jnp.where(cls == 2, 1, 2), jnp.where(cls == 1, 1, 0)
            for d in range(1, LEVEL):
                remote(carried, carried, wc_send, wc_recv.at[at], on_level(d)).start()

    put(0, 0, take(0))
    gather(0)
    deal(cls > 0)

    @pl.when(branch & carrier)
    def _():
        wait_for(carried, wo_recv)
        branch_out(carried, wo_send, wo_recv)

    share_fold((cls == 1) | (cls == 2))
    share_window(cls == 2)
    def finish():
        for step in range(2):
            part_at = lax.rem(half_at + step, 2)
            wait_for(
                turn.at[ticks, pl.ds(0, near - 1 + step), slots(ticks)],
                t_recv.at[ticks + part_at],
            )
            value = jnp.concatenate(
                [
                    turn[ticks, part_at * near + 2 * p, 1]
                    + turn[ticks, part_at * near + 2 * p + 1, 1]
                    for p in range(near // 2)
                ],
                axis=1,
            )
            lanes = pl.ds(pl.multiple_of(part_at * (size // 2), LANES), size // 2)
            sz[ticks - 1, pl.ds(place, width), lanes] = value
            part = sz.at[ticks - 1, pl.ds(place, width), lanes]
            for d in along_z:
                remote(part, part, z_send, z_recv.at[ticks - 1], on_z(d)).start()

    for n in range(ticks + 1):
        if n == ticks:
            finish()
            for k in range(ticks - 1):
                final(k)
            break
        wait_for(turn.at[n, pl.ds(0, ncol - 1), slots(n)], t_recv.at[n])
        if n == 0:
            for k in range(1, ticks):
                acc[k] = take(k)
        solved = whole(n, 1) if n > 0 else None
        if n < ticks:
            waiting = whole(n, 0)
            put(n + 1, 1, twice(nt_dot(waiting, dinv[n])))
            if n + 1 < ticks:
                value = acc[n + 1] - fold_term(n, waiting)
                if n > 0:
                    value = value - window_term(n + 1, n - 1, solved)
                put(n + 1, 0, value)
            gather(n + 1)
        if n > 0:
            sz[n - 1, pl.ds(place, width), :] = solved
            along(n - 1)
            for later in range(n + 2, ticks):
                acc[later] = acc[later] - window_term(later, n - 1, solved)
        if n == 0:
            share_fold(cls == 3)
            share_window(cls < 2)
        if n == 1:
            hand_over(range(4, 8))

            @pl.when(zed > 0)
            def _():
                remote(win, wl.at[:, cls], wl_send, wl_recv.at[1], on_twin).start()


            @pl.when(zed > 0)
            def _():
                settle()

        if n == 3:
            pass_on()
    final(ticks - 1)

    for d in range(1, LEVEL):
        to = lax.rem(cls + d, LEVEL)
        remote(usum.at[to], ub.at[cls], u_send, u_recv, on_level(d)).start()
    ub[cls] = usum[cls]
    wait_for(ub.at[pl.ds(0, LEVEL - 1)], u_recv)
    for q in range(LEVEL):
        cut = slice(q * LANES, (q + 1) * LANES)
        out_ref[:, cut] = jnp.where(zed == 0, ub[q], pend[:, cut] - ub[q])

    wait_for(recvx, x_send)
    wait_for(recvy, rs_send)
    wait_for(ub.at[pl.ds(0, LEVEL - 1)], u_send)
    wait_for(pin.at[pl.ds(0, LEVEL - 1)], sb_send)

    @pl.when(zed > 0)
    def _():
        for _ in range(3):
            wait_for(win, wl_send)

    for n in range(ticks + 1):
        wait_for(turn.at[n, pl.ds(0, ncol - 1), slots(n)], t_send.at[n])
    for k in range(ticks):
        wait_for(sz.at[k, pl.ds(0, (nz - 1) * width)], z_send)

    @pl.when(zed == 0)
    def _():
        wait_for(pt.at[:, pl.ds(0, nz - 1)], sa_send)

    @pl.when(active & (col >= lowest))
    def _():
        wait_for(ybuf.at[pl.ds(0, ncol - 1)], y_send)

    @pl.when(active)
    def _():
        wait_for(tt.at[mine, pl.ds(0, nz - 1)], tz_send)
        for _ in range(LEVEL - 1):
            wait_for(tt.at[mine], ts_send)

    @pl.when(active & (zed == 0))
    def _():
        for _ in trunk:
            wait_for(wc.at[mine, mine], wr_send)

    @pl.when(carrier & (zed == 0))
    def _():
        for _ in trunk:
            wait_for(carried, wo_send)

    @pl.when(active & branch)
    def _():
        for _ in range(2):
            wait_for(wc.at[mine, mine], wr_send)

    @pl.when(carrier & branch)
    def _():
        for _ in range(2):
            wait_for(carried, wo_send)

    @pl.when((zed == 0) & (cls == LEVEL - 1))
    def _():
        wait_for(wc.at[2, pl.ds(0, 2)], wh_send)

    @pl.when(carrier)
    def _():
        wait_for(wc.at[0], wc_send)


def per_device(right_side, prior_panel, prior_solved, window_panel, diag_inverse):
    rows, columns = right_side.shape[2:]
    size = prior_panel.shape[4]
    ticks = window_panel.shape[2]
    ncol = lax.axis_size("col")
    nz = lax.axis_size("row") // LEVEL
    width = LANES // nz
    near = ncol // 2
    dma = pltpu.SemaphoreType.DMA
    vmem = pltpu.VMEM
    out = pl.pallas_call(
        functools.partial(kernel, nz, ncol),
        out_shape=jax.ShapeDtypeStruct((rows, columns), F32),
        in_specs=[pl.BlockSpec(memory_space=pl.ANY)] * 5,
        out_specs=pl.BlockSpec(memory_space=pltpu.VMEM),
        scratch_shapes=[
            vmem((rows, columns), F32),
            vmem((size, size), BF16),
            vmem((size, columns), BF16),
            vmem((ticks, rows, size), BF16),
            vmem((ticks, rows, size), BF16),
            vmem((near, rows, columns), BF16),
            vmem((near, rows, columns), BF16),
            vmem((near, rows, columns), F32),
            vmem((near, rows, columns), BF16),
            vmem((near - 1, rows, columns), BF16),
            vmem((rows, columns), F32),
            vmem((LEVEL, nz, width, LANES), BF16),
            vmem((LEVEL, width, LANES), BF16),
            vmem((LEVEL, width, LANES), BF16),
            vmem((ticks, width, LANES), F32),
            vmem((ticks + 1, ncol, 2, width, LANES), BF16),
            vmem((ticks, LANES, size), BF16),
            vmem((ticks, LEVEL, rows, size), BF16),
            vmem((LEVEL - 1, LEVEL - 1, rows, size), BF16),
            vmem((ncol, rows, LANES), BF16),
            vmem((LEVEL - 1, nz, rows, LANES), BF16),
            vmem((LEVEL, rows, LANES), F32),
            vmem((LEVEL, rows, LANES), F32),
            dma((5,)),
            dma,
            dma((near,)),
            dma,
            dma,
            dma,
            dma,
            dma,
            dma((LEVEL,)),
            dma,
            dma,
            dma,
            dma,
            dma,
            dma,
            dma,
            dma((LEVEL - 1, LEVEL - 1)),
            dma,
            dma((3,)),
            dma,
            dma((ncol,)),
            dma,
            dma,
            dma,
            dma((LEVEL - 1,)),
            dma((ticks + 1,)),
            dma((ticks + 2,)),
            dma,
            dma((ticks,)),
            dma,
            dma,
        ],
        compiler_params=pltpu.CompilerParams(
            collective_id=0,
            has_side_effects=True,
            vmem_limit_bytes=55040 * 1024,
        ),
    )(
        right_side.reshape(rows, columns),
        prior_panel.reshape(size, size),
        prior_solved.reshape(size, columns),
        window_panel.reshape(ticks, rows, size),
        diag_inverse,
    )
    return out.reshape(right_side.shape)


def solution(mesh):
    return jax.shard_map(
        per_device,
        mesh=mesh,
        in_specs=(
            P(None, "row", "col", None),
            P(None, "row", None, "col", None, None),
            P(None, "col", None, None),
            P(None, "row", None, "col", None),
            P(None, "col", None),
        ),
        out_specs=P(None, "row", "col", None),
        check_vma=False,
    )
```
